512 devices in a mesh: gx: 8 (over x, z_hi), gy: 8 (over y, core), gz: 8 (over z_lo).
Axes of the slice: x: 4, y: 4, z: 16 (z_hi: 2, z_lo: 8; z = z_hi * 8 + z_lo), core: 2. Of those that a mesh axis runs over, the one named last changes fastest.
Arguments:
- tokens: bfloat16 [256, 12288], P(('gx', 'gy'), 'gz'), may hold values from -6 to 6
- up_proj: bfloat16 [12288, 24576], P(None, ('gx', 'gy', 'gz')), may hold values from -0.0546875 to 0.0546875
- down_proj: bfloat16 [24576, 12288], P(('gx', 'gy', 'gz')), may hold values from -0.0390625 to 0.0390625
- out_grad: bfloat16 [256, 12288], P(('gx', 'gy'), 'gz'), may hold values from -6 to 6
Outputs:
- output: bfloat16 [256, 12288], P(('gx', 'gy'), 'gz')
- input_grad: bfloat16 [256, 12288], P(('gx', 'gy'), 'gz')
- up_grad: bfloat16 [12288, 24576], P('gz', ('gx', 'gy'))
- down_grad: bfloat16 [24576, 12288], P(('gx', 'gy'), 'gz')
The draws below stay inside these ranges and needn't reach their ends.
All inputs are finite; a program needn't handle non-finite values.
Results may differ from the reference program's by a relative error of at most 0.0049.
Values may be sent and summed in bfloat16 or wider, within the bound.
No kernel may reach another device: no remote copies, remote signals or barrier semaphores. Data moves between devices by JAX's collectives and lax.ppermute only.
A program may use at most 64 MiB of HBM per device.

```python
import jax
import jax.numpy as jnp

D = 12288
FF = 24576
TOKENS = 256


def level_of(key, extent, split, smallest, largest):
    def one(axis_at, shards_of):
        steps = jax.random.uniform(jax.random.fold_in(jax.random.fold_in(key, 6), axis_at), (shards_of,), jnp.float32, smallest / len(split), largest / len(split))
        return jnp.repeat(jnp.exp(steps), extent[axis_at] // shards_of).reshape((-1,) + (1,) * (len(extent) - axis_at - 1))

    level = one(*split[0])
    for cut in split[1:]:
        level = level * one(*cut)
    return level


def bell_draw(stream_key, shape, spread, bound, pieces=(), held_as=jnp.bfloat16):
    array = spread * jax.random.normal(stream_key, shape, jnp.float32)
    if pieces:
        array = array * level_of(stream_key, shape, pieces, -0.22, 0.18)
    return jnp.clip(array, -bound, bound).astype(held_as)


def setup_inputs(seed: int = 0) -> dict:
    streams_of = jax.random.split(jax.random.key(seed), 5)
    return {
        "tokens": bell_draw(streams_of[0], (TOKENS, D), 1.0, 6.0, ((0, 64), (1, 8))),
        "up_proj": bell_draw(streams_of[1], (D, FF), D ** -0.5, 0.0546875, ((1, 512),)),
        "down_proj": bell_draw(streams_of[2], (FF, D), FF ** -0.5, 0.0390625, ((0, 512),)),
        "out_grad": bell_draw(streams_of[3], (TOKENS, D), 1.0, 6.0, ((0, 64), (1, 8))),
    }


def activate(values):
    return jax.nn.gelu(values, approximate=True)

def reference(tokens, up_proj, down_proj, out_grad):
    pre_act = jnp.dot(tokens, up_proj, preferred_element_type=jnp.float32)
    acted = activate(pre_act).astype(jnp.bfloat16)
    output = jnp.dot(acted, down_proj, preferred_element_type=jnp.float32).astype(jnp.bfloat16)
    down_grad = jnp.dot(acted.T, out_grad, preferred_element_type=jnp.float32).astype(jnp.bfloat16)
    act_grad = jnp.dot(out_grad, down_proj.T, preferred_element_type=jnp.float32)
    unused, pullback = jax.vjp(activate, pre_act)
    pre_grad = pullback(act_grad)[0].astype(jnp.bfloat16)
    up_grad = jnp.dot(tokens.T, pre_grad, preferred_element_type=jnp.float32).astype(jnp.bfloat16)
    input_grad = jnp.dot(pre_grad, up_proj.T, preferred_element_type=jnp.float32).astype(jnp.bfloat16)
    return (output, input_grad, up_grad, down_grad)
```

```python
import jax
import jax.numpy as jnp
from jax import lax
from jax.sharding import Mesh, PartitionSpec as P

BF16 = jnp.bfloat16
F32 = jnp.float32


def activate(values):
    return jax.nn.gelu(values, approximate=True)


def gelu_slope(pre_act, cotangent):
    unused, pullback = jax.vjp(activate, pre_act)
    return pullback(cotangent)[0]


def exchange(value, axes):
    return lax.all_to_all(value, axes, split_axis=0, concat_axis=0, tiled=True)


def spread(value, axes, count):
    return exchange(jnp.broadcast_to(value[None], (count,) + value.shape), axes)


def other_core(value):
    return lax.ppermute(value, "c", [(0, 1), (1, 0)])


def dot(left, right, left_dim, right_dim):
    return lax.dot_general(
        left, right, (((left_dim,), (right_dim,)), ((), ())), preferred_element_type=F32
    )


PLANE = ("xh", "xp", "y")
COLUMN = ("zh", "z2", "z1")
GROUP = ("xp", "zp")
LINE = ("z2", "z1", "zp")


def local(tokens, up_proj, down_proj, out_grad):
    width = tokens.shape[1]
    units = down_proj.shape[0]

    def regroup(weight):
        blocks = weight.reshape(units, 2, 2, 2, width)
        sent = blocks.transpose(2, 3, 0, 1, 4)
        own = exchange(sent.reshape(4, units, 2 * width), GROUP)
        own = own.reshape(4 * units, 2 * width)
        return own, other_core(own)

    both = jnp.concatenate([tokens, out_grad], axis=0)
    column = spread(both, COLUMN, 8).reshape(2, 2, 2, 2, 4, width)
    sent = column.transpose(2, 1, 3, 0, 4, 5).reshape(1, 2, 1, 2, 2, 8, width)
    sent = jnp.broadcast_to(sent, (2, 2, 4, 2, 2, 8, width)).reshape(16, 2, 2, 8, width)
    plane = exchange(sent, PLANE)
    rows = plane.transpose(2, 0, 3, 1, 4).reshape(2, 128, 2 * width)

    up = regroup(up_proj.T)
    down = regroup(down_proj)

    parts = jnp.stack(
        [
            jnp.stack([dot(weight, rows[at], 1, 1).reshape(4, units, 128) for weight in pair], 1)
            for at, pair in ((0, up), (1, down))
        ],
        1,
    )
    sums = jnp.sum(exchange(parts, GROUP).reshape(4, 2, 2, units, 128), axis=0)
    acted = activate(sums[0]).astype(BF16)
    pre_grad = gelu_slope(sums[0], sums[1]).astype(BF16)
    hidden = jnp.stack([acted, pre_grad])
    shared = spread(hidden, GROUP, 4).reshape(4, 2, 2, units, 128)

    def partial_rows(kind, pair):
        total = sum(
            dot(shared[:, kind, at].reshape(4 * units, 128), pair[at], 0, 0) for at in range(2)
        )
        return total.astype(BF16).reshape(16, 8, 2 * width)

    partials = jnp.stack([partial_rows(0, down), partial_rows(1, up)], 1)
    arrived = exchange(partials, PLANE).reshape(2, 2, 4, 2, 8, 2 * width)
    summed = jnp.sum(arrived.astype(F32), axis=(0, 2))
    summed = summed.astype(BF16).reshape(2, 2, 2, 4, 2, width)
    summed = summed.transpose(2, 4, 0, 1, 3, 5).reshape(8, 2, 4, width)
    ends = jnp.sum(exchange(summed, COLUMN).astype(F32), axis=0).astype(BF16)

    mine = lax.dynamic_index_in_dim(
        column.reshape(2, 4, 2, 4, width), lax.axis_index(("z2", "z1")), 1, keepdims=False
    )
    mine = mine.transpose(1, 0, 2, 3).reshape(2, 8, width)
    flat = spread(mine, PLANE, 16).reshape(16, 2, 8, width).transpose(1, 0, 2, 3).reshape(2, 128, width)
    flat = jnp.concatenate([flat, other_core(flat)], axis=1)
    units_all = jnp.concatenate([hidden[:, 0], other_core(hidden[:, 1])], axis=2)
    units_all = spread(units_all, LINE, 8).reshape(8, 2, units, 256)
    down_grad = dot(units_all[:, 0].reshape(8 * units, 256), flat[1], 1, 0).astype(BF16)
    up_grad = dot(flat[0], units_all[:, 1].reshape(8 * units, 256), 0, 1).astype(BF16)
    return (ends[0], ends[1], up_grad, down_grad)


def solution(mesh):
    fine = Mesh(
        mesh.devices.reshape(2, 2, 2, 4, 2, 2, 2, 2),
        ("xh", "xp", "zh", "y", "c", "z2", "z1", "zp"),
    )
    owners = ("xh", "xp", "zh", "y", "c")
    features = ("z2", "z1", "zp")
    return jax.shard_map(
        local,
        mesh=fine,
        in_specs=(
            P(owners, features),
            P(None, owners + features),
            P(owners + features, None),
            P(owners, features),
        ),
        out_specs=(
            P(owners, features),
            P(owners, features),
            P(features, owners),
            P(owners, features),
        ),
        check_vma=False,
    )
```

```python
import jax
import jax.numpy as jnp
from jax import lax
from jax.experimental import pallas as pl
from jax.experimental.pallas import tpu as pltpu
from jax.sharding import Mesh, PartitionSpec as P

BF16 = jnp.bfloat16
F32 = jnp.float32
VMEM_BYTES = 48 * 1024 * 1024

PLANE = ("xh", "xp", "y")
COLUMN = ("zh", "z2", "z1")
GROUP = ("xp", "zp")


def activate(values):
    return jax.nn.gelu(values, approximate=True)


def gelu_slope(pre_act, cotangent):
    unused, pullback = jax.vjp(activate, pre_act)
    return pullback(cotangent)[0]


def exchange(value, axes):
    return lax.all_to_all(value, axes, split_axis=0, concat_axis=0, tiled=True)


def spread(value, axes, count):
    return exchange(jnp.broadcast_to(value[None], (count,) + value.shape), axes)


def partner(value, axes, count, step):
    return lax.ppermute(value, axes, [(at, at ^ step) for at in range(count)])


def other_core(value):
    return partner(value, "c", 2, 1)


def gather_ring(value, axes, count, dim):
    here = lax.axis_index(axes)
    shape = list(value.shape)
    shape[dim] = count
    start = [0] * len(shape)
    whole = jnp.zeros(shape, value.dtype)
    for step in range(count):
        block = partner(value, axes, count, step) if step else value
        start[dim] = here ^ step
        whole = lax.dynamic_update_slice(whole, block, tuple(start))
    return whole


def after(value, *others):
    return lax.optimization_barrier((value,) + others)[0]


def dot(left, right, left_dim, right_dim):
    return lax.dot_general(
        left, right, (((left_dim,), (right_dim,)), ((), ())), preferred_element_type=F32
    )


def cut_kernel(member_ref, up_ref, down_ref, *refs):
    pieces, sems = refs[:4], refs[4]
    width = pieces[0].shape[2] // 2
    copies = []
    for step in range(4):
        for kind, source in enumerate((up_ref, down_ref)):
            for far in range(2):
                column = pl.multiple_of((far * 4 + (member_ref[0] ^ step)) * width, width)
                copies.append(
                    pltpu.make_async_copy(
                        source.at[:, pl.ds(column, width)],
                        pieces[step].at[kind, :, pl.ds(far * width, width)],
                        sems.at[len(copies)],
                    )
                )
                copies[-1].start()
    for copy in copies:
        copy.wait()


def cut(member, up_rows, down_rows):
    units, features = up_rows.shape
    piece = jax.ShapeDtypeStruct((2, units, features // 4), BF16)
    return pl.pallas_call(
        cut_kernel,
        out_shape=[piece] * 4,
        in_specs=[pl.BlockSpec(memory_space=pltpu.SMEM)] + [pl.BlockSpec(memory_space=pl.ANY)] * 2,
        out_specs=[pl.BlockSpec(memory_space=pl.ANY)] * 4,
        scratch_shapes=[pltpu.SemaphoreType.DMA((16,))],
        cost_estimate=pl.CostEstimate(flops=0, bytes_accessed=16 * units * features, transcendentals=0),
        name="cut_weights",
    )(member, up_rows, down_rows)


def hidden_kernel(member_ref, rows_ref, *refs):
    own, beside, out_ref = refs[:4], refs[4:8], refs[8]
    units = own[0].shape[1]
    width = rows_ref.shape[4]
    for kind in range(2):
        rows = [rows_ref[:, far, kind].reshape(-1, width) for far in range(2)]
        for core, pieces in enumerate((own, beside)):
            total = None
            for far in range(2):
                weight = jnp.concatenate(
                    [piece[kind, :, far * width : (far + 1) * width] for piece in pieces], axis=0
                )
                term = dot(weight, rows[far], 1, 1)
                total = term if total is None else total + term
            for step in range(4):
                out_ref[member_ref[0] ^ step, kind, core] = total[step * units : (step + 1) * units]


def hidden_parts(member, rows, own, beside):
    units = own[0].shape[1]
    tokens = rows.shape[0] * rows.shape[3]
    return pl.pallas_call(
        hidden_kernel,
        out_shape=jax.ShapeDtypeStruct((4, 2, 2, units, tokens), F32),
        in_specs=[pl.BlockSpec(memory_space=pltpu.SMEM)] + [pl.BlockSpec(memory_space=pltpu.VMEM)] * 9,
        out_specs=pl.BlockSpec(memory_space=pltpu.VMEM),
        compiler_params=pltpu.CompilerParams(vmem_limit_bytes=VMEM_BYTES),
        cost_estimate=pl.CostEstimate(flops=604_000_000, bytes_accessed=6_700_000, transcendentals=0),
        name="hidden_parts",
    )(member, rows, *own, *beside)


def gelu_kernel(parts_ref, own_ref, spread_ref):
    pre_act = parts_ref[0, 0] + parts_ref[1, 0] + parts_ref[2, 0] + parts_ref[3, 0]
    act_grad = parts_ref[0, 1] + parts_ref[1, 1] + parts_ref[2, 1] + parts_ref[3, 1]
    for kind, value in enumerate((activate(pre_act), gelu_slope(pre_act, act_grad))):
        value = value.astype(BF16)
        own_ref[kind] = value
        for at in range(4):
            spread_ref[at, kind] = value


def gelu_both(parts):
    shape = parts.shape
    return pl.pallas_call(
        gelu_kernel,
        out_shape=[jax.ShapeDtypeStruct(shape[1:], BF16), jax.ShapeDtypeStruct(shape, BF16)],
        in_specs=[pl.BlockSpec(memory_space=pltpu.VMEM)],
        out_specs=[pl.BlockSpec(memory_space=pltpu.VMEM)] * 2,
        cost_estimate=pl.CostEstimate(flops=1_000_000, bytes_accessed=700_000, transcendentals=12_288),
        name="gelu_both",
    )(parts)


def output_kernel(member_ref, shared_ref, *refs):
    own, beside, out_ref = refs[:4], refs[4:8], refs[8]
    features = own[0].shape[2]
    count, unused, rows, unused = out_ref.shape
    step_of = features // 4
    for result in range(2):
        units = jnp.concatenate(
            [shared_ref[member_ref[0] ^ step, result, core] for core in range(2) for step in range(4)],
            axis=0,
        )
        for at in range(4):
            columns = slice(at * step_of, (at + 1) * step_of)
            weight = jnp.concatenate(
                [piece[1 - result, :, columns] for piece in (*own, *beside)], axis=0
            )
            total = dot(units, weight, 0, 0)
            out_ref[:, result, :, columns] = total.astype(BF16).reshape(count, rows, step_of)


def output_parts(member, shared, own, beside, count):
    features = own[0].shape[2]
    rows = shared.shape[4] // count
    return pl.pallas_call(
        output_kernel,
        out_shape=jax.ShapeDtypeStruct((count, 2, rows, features), BF16),
        in_specs=[pl.BlockSpec(memory_space=pltpu.SMEM)] + [pl.BlockSpec(memory_space=pltpu.VMEM)] * 9,
        out_specs=pl.BlockSpec(memory_space=pltpu.VMEM),
        compiler_params=pltpu.CompilerParams(vmem_limit_bytes=VMEM_BYTES),
        cost_estimate=pl.CostEstimate(flops=604_000_000, bytes_accessed=6_700_000, transcendentals=0),
        name="output_parts",
    )(member, shared, *own, *beside)


def local(tokens, up_proj, down_proj, out_grad):
    width = tokens.shape[1]
    units = down_proj.shape[0]
    member = lax.axis_index(GROUP).reshape(1).astype(jnp.int32)

    both = jnp.concatenate([tokens, out_grad], axis=0)
    column = spread(both, COLUMN, 8).reshape(2, 2, 2, 2, 4, width)
    sent = column.transpose(2, 1, 3, 0, 4, 5).reshape(1, 2, 1, 2, 2, 8, width)
    sent = jnp.broadcast_to(sent, (2, 2, 4, 2, 2, 8, width)).reshape(16, 2, 2, 8, width)
    plane = exchange(sent, PLANE)

    pieces = cut(member, up_proj.T, down_proj)
    own = [pieces[0]] + [partner(pieces[step], GROUP, 4, step) for step in range(1, 4)]
    beside = [other_core(piece) for piece in own]

    parts = hidden_parts(member, plane, own, beside)
    hidden, shared = gelu_both(exchange(parts, GROUP))
    shared = exchange(shared, GROUP)

    partials = output_parts(member, shared, own, beside, 16)
    arrived = exchange(partials, PLANE)
    summed = jnp.sum(arrived.reshape(2, 2, 4, 2, 8, 2 * width).astype(F32), axis=(0, 2))
    summed = summed.astype(BF16).reshape(2, 2, 2, 4, 2, width)
    summed = summed.transpose(2, 4, 0, 1, 3, 5).reshape(8, 2, 4, width)
    ends = jnp.sum(exchange(summed, COLUMN).astype(F32), axis=0).astype(BF16)

    mine = lax.dynamic_index_in_dim(
        column.reshape(2, 4, 2, 4, width), lax.axis_index(("z2", "z1")), 1, keepdims=False
    )
    mine = mine.transpose(1, 0, 2, 3).reshape(2, 1, 1, 8, width)
    flat = gather_ring(mine, "y", 4, 2)
    flat = gather_ring(after(flat, partials), ("xh", "xp"), 4, 1).reshape(2, 128, width)
    flat = jnp.concatenate([flat, other_core(flat)], axis=1)
    units_all = jnp.concatenate([hidden[:, 0], other_core(hidden[:, 1])], axis=2)
    units_all = gather_ring(after(units_all, partials)[:, None], "z2", 2, 1)
    units_all = gather_ring(units_all[:, :, None], "z1", 2, 2)
    units_all = gather_ring(after(units_all, arrived)[:, :, :, None], "zp", 2, 3)
    units_all = units_all.reshape(2, 8 * units, 256)
    down_grad = dot(units_all[0], flat[1], 1, 0).astype(BF16)
    up_grad = dot(flat[0], units_all[1], 0, 1).astype(BF16)
    return (ends[0], ends[1], up_grad, down_grad)


def solution(mesh):
    fine = Mesh(
        mesh.devices.reshape(2, 2, 2, 4, 2, 2, 2, 2),
        ("xh", "xp", "zh", "y", "c", "z2", "z1", "zp"),
    )
    owners = ("xh", "xp", "zh", "y", "c")
    features = ("z2", "z1", "zp")
    return jax.shard_map(
        local,
        mesh=fine,
        in_specs=(
            P(owners, features),
            P(None, owners + features),
            P(owners + features, None),
            P(owners, features),
        ),
        out_specs=(
            P(owners, features),
            P(owners, features),
            P(features, owners),
            P(owners, features),
        ),
        check_vma=False,
    )
```

```python
import jax
import jax.numpy as jnp
from jax import lax
from jax.experimental import pallas as pl
from jax.experimental.pallas import tpu as pltpu
from jax.sharding import Mesh, PartitionSpec as P

BF16 = jnp.bfloat16
F32 = jnp.float32
VMEM_BYTES = 48 * 1024 * 1024

PLANE = ("xh", "xp", "y")
COLUMN = ("zh", "z2", "z1")
GROUP = ("xp", "zp")


def activate(values):
    return jax.nn.gelu(values, approximate=True)


def gelu_slope(pre_act, cotangent):
    unused, pullback = jax.vjp(activate, pre_act)
    return pullback(cotangent)[0]


def exchange(value, axes):
    return lax.all_to_all(value, axes, split_axis=0, concat_axis=0, tiled=True)


def spread(value, axes, count):
    return exchange(jnp.broadcast_to(value[None], (count,) + value.shape), axes)


def partner(value, axes, count, step):
    return lax.ppermute(value, axes, [(at, at ^ step) for at in range(count)])


def other_core(value):
    return partner(value, "c", 2, 1)


def gather_ring(value, axes, count, dim):
    here = lax.axis_index(axes)
    shape = list(value.shape)
    shape[dim] = count
    start = [0] * len(shape)
    whole = jnp.zeros(shape, value.dtype)
    blocks = [value] + [partner(value, axes, count, step) for step in range(1, count)]
    for step, block in enumerate(lax.optimization_barrier(blocks)):
        start[dim] = here ^ step
        whole = lax.dynamic_update_slice(whole, block, tuple(start))
    return whole


def after(value, *others):
    return lax.optimization_barrier((value,) + others)[0]


def dot(left, right, left_dim, right_dim):
    return lax.dot_general(
        left, right, (((left_dim,), (right_dim,)), ((), ())), preferred_element_type=F32
    )


def cut_kernel(member_ref, up_ref, down_ref, *pieces):
    width = pieces[0].shape[2] // 2
    for step in range(4):
        for kind, source in enumerate((up_ref, down_ref)):
            for far in range(2):
                column = pl.multiple_of((far * 4 + (member_ref[0] ^ step)) * width, width)
                pieces[step][kind, :, far * width : (far + 1) * width] = source[:, pl.ds(column, width)]


def cut(member, up_rows, down_rows):
    units, features = up_rows.shape
    piece = jax.ShapeDtypeStruct((2, units, features // 4), BF16)
    return pl.pallas_call(
        cut_kernel,
        out_shape=[piece] * 4,
        in_specs=[pl.BlockSpec(memory_space=pltpu.SMEM)] + [pl.BlockSpec(memory_space=pltpu.VMEM)] * 2,
        out_specs=[pl.BlockSpec(memory_space=pltpu.VMEM)] * 4,
        compiler_params=pltpu.CompilerParams(vmem_limit_bytes=VMEM_BYTES),
        cost_estimate=pl.CostEstimate(flops=0, bytes_accessed=8 * units * features, transcendentals=0),
        name="cut_weights",
    )(member, up_rows, down_rows)


def hidden_kernel(member_ref, rows_ref, *refs):
    own, beside, out_ref = refs[:4], refs[4:8], refs[8]
    units = own[0].shape[1]
    width = rows_ref.shape[4]
    for kind in range(2):
        rows = [rows_ref[:, far, kind].reshape(-1, width) for far in range(2)]
        for core, pieces in enumerate((own, beside)):
            total = None
            for far in range(2):
                weight = jnp.concatenate(
                    [piece[kind, :, far * width : (far + 1) * width] for piece in pieces], axis=0
                )
                term = dot(weight, rows[far], 1, 1)
                total = term if total is None else total + term
            for step in range(4):
                out_ref[member_ref[0] ^ step, kind, core] = total[step * units : (step + 1) * units]


def hidden_parts(member, rows, own, beside):
    units = own[0].shape[1]
    tokens = rows.shape[0] * rows.shape[3]
    return pl.pallas_call(
        hidden_kernel,
        out_shape=jax.ShapeDtypeStruct((4, 2, 2, units, tokens), F32),
        in_specs=[pl.BlockSpec(memory_space=pltpu.SMEM)] + [pl.BlockSpec(memory_space=pltpu.VMEM)] * 9,
        out_specs=pl.BlockSpec(memory_space=pltpu.VMEM),
        compiler_params=pltpu.CompilerParams(vmem_limit_bytes=VMEM_BYTES),
        cost_estimate=pl.CostEstimate(flops=604_000_000, bytes_accessed=6_700_000, transcendentals=0),
        name="hidden_parts",
    )(member, rows, *own, *beside)


def gelu_kernel(parts_ref, own_ref, spread_ref):
    pre_act = parts_ref[0, 0] + parts_ref[1, 0] + parts_ref[2, 0] + parts_ref[3, 0]
    act_grad = parts_ref[0, 1] + parts_ref[1, 1] + parts_ref[2, 1] + parts_ref[3, 1]
    for kind, value in enumerate((activate(pre_act), gelu_slope(pre_act, act_grad))):
        value = value.astype(BF16)
        own_ref[kind] = value
        for at in range(4):
            spread_ref[at, kind] = value


def gelu_both(parts):
    shape = parts.shape
    return pl.pallas_call(
        gelu_kernel,
        out_shape=[jax.ShapeDtypeStruct(shape[1:], BF16), jax.ShapeDtypeStruct(shape, BF16)],
        in_specs=[pl.BlockSpec(memory_space=pltpu.VMEM)],
        out_specs=[pl.BlockSpec(memory_space=pltpu.VMEM)] * 2,
        cost_estimate=pl.CostEstimate(flops=1_000_000, bytes_accessed=700_000, transcendentals=12_288),
        name="gelu_both",
    )(parts)


def output_kernel(member_ref, shared_ref, *refs):
    own, beside, out_ref = refs[:4], refs[4:8], refs[8]
    features = own[0].shape[2]
    count, unused, rows, unused = out_ref.shape
    step_of = features // 4
    for result in range(2):
        units = jnp.concatenate(
            [shared_ref[member_ref[0] ^ step, result, core] for core in range(2) for step in range(4)],
            axis=0,
        )
        for at in range(4):
            columns = slice(at * step_of, (at + 1) * step_of)
            weight = jnp.concatenate(
                [piece[1 - result, :, columns] for piece in (*own, *beside)], axis=0
            )
            total = dot(units, weight, 0, 0)
            out_ref[:, result, :, columns] = total.astype(BF16).reshape(count, rows, step_of)


def output_parts(member, shared, own, beside, count):
    features = own[0].shape[2]
    rows = shared.shape[4] // count
    return pl.pallas_call(
        output_kernel,
        out_shape=jax.ShapeDtypeStruct((count, 2, rows, features), BF16),
        in_specs=[pl.BlockSpec(memory_space=pltpu.SMEM)] + [pl.BlockSpec(memory_space=pltpu.VMEM)] * 9,
        out_specs=pl.BlockSpec(memory_space=pltpu.VMEM),
        compiler_params=pltpu.CompilerParams(vmem_limit_bytes=VMEM_BYTES),
        cost_estimate=pl.CostEstimate(flops=604_000_000, bytes_accessed=6_700_000, transcendentals=0),
        name="output_parts",
    )(member, shared, *own, *beside)


def local(tokens, up_proj, down_proj, out_grad):
    width = tokens.shape[1]
    units = down_proj.shape[0]
    member = lax.axis_index(GROUP).reshape(1).astype(jnp.int32)

    pieces = cut(member, up_proj.T, down_proj)
    own = [pieces[0]] + [partner(pieces[step], GROUP, 4, step) for step in range(1, 4)]
    beside = [other_core(piece) for piece in own]

    both = jnp.concatenate([tokens, out_grad], axis=0)
    column = spread(both, COLUMN, 8).reshape(2, 2, 2, 2, 4, width)
    sent = column.transpose(2, 1, 3, 0, 4, 5).reshape(1, 2, 1, 2, 2, 8, width)
    sent = jnp.broadcast_to(sent, (2, 2, 4, 2, 2, 8, width)).reshape(16, 2, 2, 8, width)
    plane = exchange(after(sent, *own), PLANE)

    mine = lax.dynamic_index_in_dim(
        column.reshape(2, 4, 2, 4, width), lax.axis_index(("z2", "z1")), 1, keepdims=False
    )
    mine = mine.transpose(1, 0, 2, 3).reshape(2, 1, 1, 8, width)
    flat = gather_ring(mine, "y", 4, 2)
    flat = gather_ring(flat, ("xh", "xp"), 4, 1).reshape(2, 128, width)

    parts = hidden_parts(after(member, flat), plane, own, beside)
    hidden, shared = gelu_both(exchange(parts, GROUP))
    shared = exchange(shared, GROUP)

    partials = output_parts(member, shared, own, beside, 16)
    arrived = exchange(partials, PLANE)
    summed = jnp.sum(arrived.reshape(2, 2, 4, 2, 8, 2 * width).astype(F32), axis=(0, 2))
    summed = summed.astype(BF16).reshape(2, 2, 2, 4, 2, width)
    summed = summed.transpose(2, 4, 0, 1, 3, 5).reshape(8, 2, 4, width)
    ends = jnp.sum(exchange(summed, COLUMN).astype(F32), axis=0).astype(BF16)

    flat = jnp.concatenate([flat, other_core(flat)], axis=1)
    lines = lax.dynamic_slice_in_dim(shared, member[0] // 2 * 2, 2, 0)[None, None]
    lines = gather_ring(after(lines, partials), "z2", 2, 0)
    lines = gather_ring(lines, "z1", 2, 1)
    lines = after(lines, arrived).transpose(4, 3, 0, 1, 2, 5, 6).reshape(2, 2, 8 * units, 128)
    units_all = jnp.concatenate([lines[0], other_core(lines[1])], axis=2)
    down_grad = dot(units_all[0], flat[1], 1, 0).astype(BF16)
    up_grad = dot(flat[0], units_all[1], 0, 1).astype(BF16)
    return (ends[0], ends[1], up_grad, down_grad)


def solution(mesh):
    fine = Mesh(
        mesh.devices.reshape(2, 2, 2, 4, 2, 2, 2, 2),
        ("xh", "xp", "zh", "y", "c", "z2", "z1", "zp"),
    )
    owners = ("xh", "xp", "zh", "y", "c")
    features = ("z2", "z1", "zp")
    return jax.shard_map(
        local,
        mesh=fine,
        in_specs=(
            P(owners, features),
            P(None, owners + features),
            P(owners + features, None),
            P(owners, features),
        ),
        out_specs=(
            P(owners, features),
            P(owners, features),
            P(features, owners),
            P(owners, features),
        ),
        check_vma=False,
    )
```

```python
import jax
import jax.numpy as jnp
from jax import lax
from jax.experimental import pallas as pl
from jax.experimental.pallas import tpu as pltpu
from jax.sharding import Mesh, PartitionSpec as P

BF16 = jnp.bfloat16
F32 = jnp.float32
VMEM_BYTES = 20 * 1024 * 1024

PLANE = ("xh", "xp", "y")
COLUMN = ("zh", "z2", "z1")
GROUP = ("xp", "zp")


def activate(values):
    return jax.nn.gelu(values, approximate=True)


def gelu_slope(pre_act, cotangent):
    unused, pullback = jax.vjp(activate, pre_act)
    return pullback(cotangent)[0]


def exchange(value, axes):
    return lax.all_to_all(value, axes, split_axis=0, concat_axis=0, tiled=True)


def spread(value, axes, count):
    return exchange(jnp.broadcast_to(value[None], (count,) + value.shape), axes)


def partner(value, axes, count, step):
    return lax.ppermute(value, axes, [(at, at ^ step) for at in range(count)])


def other_core(value):
    return partner(value, "c", 2, 1)


def gather_ring(value, axes, count, dim):
    here = lax.axis_index(axes)
    shape = list(value.shape)
    shape[dim] = count
    start = [0] * len(shape)
    whole = jnp.zeros(shape, value.dtype)
    blocks = [value] + [partner(value, axes, count, step) for step in range(1, count)]
    for step, block in enumerate(lax.optimization_barrier(blocks)):
        start[dim] = here ^ step
        whole = lax.dynamic_update_slice(whole, block, tuple(start))
    return whole


def after(value, *others):
    return lax.optimization_barrier((value,) + others)[0]


def dot(left, right, left_dim, right_dim):
    return lax.dot_general(
        left, right, (((left_dim,), (right_dim,)), ((), ())), preferred_element_type=F32
    )


def cut_kernel(member_ref, up_ref, down_ref, *pieces):
    width = pieces[0].shape[2] // 2
    for step in range(4):
        for kind, source in enumerate((up_ref, down_ref)):
            for far in range(2):
                column = pl.multiple_of((far * 4 + (member_ref[0] ^ step)) * width, width)
                pieces[step][kind, :, far * width : (far + 1) * width] = source[:, pl.ds(column, width)]


def cut(member, up_rows, down_rows):
    units, features = up_rows.shape
    piece = jax.ShapeDtypeStruct((2, units, features // 4), BF16)
    return pl.pallas_call(
        cut_kernel,
        out_shape=[piece] * 4,
        in_specs=[pl.BlockSpec(memory_space=pltpu.SMEM)] + [pl.BlockSpec(memory_space=pltpu.VMEM)] * 2,
        out_specs=[pl.BlockSpec(memory_space=pltpu.VMEM)] * 4,
        compiler_params=pltpu.CompilerParams(vmem_limit_bytes=VMEM_BYTES),
        cost_estimate=pl.CostEstimate(flops=0, bytes_accessed=8 * units * features, transcendentals=0),
        name="cut_weights",
    )(member, up_rows, down_rows)


def lay_out_kernel(block_ref, column_ref, sent_ref, mine_ref):
    for far in range(2):
        for near in range(2):
            ends = [column_ref[end * 4 + far * 2 + near].astype(F32) for end in range(2)]
            for array in range(2):
                rows = jnp.concatenate([end[array * 4 : array * 4 + 4] for end in ends], axis=0).astype(BF16)
                for half in range(2):
                    for line in range(4):
                        sent_ref[half * 8 + near * 4 + line, far, array] = rows
    ends = [column_ref[end * 4 + block_ref[0]].astype(F32) for end in range(2)]
    for array in range(2):
        rows = jnp.concatenate([end[array * 4 : array * 4 + 4] for end in ends], axis=0)
        mine_ref[array, 0, 0] = rows.astype(BF16)


def lay_out(block, column):
    unused, rows, width = column.shape
    return pl.pallas_call(
        lay_out_kernel,
        out_shape=[
            jax.ShapeDtypeStruct((16, 2, 2, rows, width), BF16),
            jax.ShapeDtypeStruct((2, 1, 1, rows, width), BF16),
        ],
        in_specs=[pl.BlockSpec(memory_space=pltpu.SMEM), pl.BlockSpec(memory_space=pltpu.VMEM)],
        out_specs=[pl.BlockSpec(memory_space=pltpu.VMEM)] * 2,
        compiler_params=pltpu.CompilerParams(vmem_limit_bytes=VMEM_BYTES),
        cost_estimate=pl.CostEstimate(flops=0, bytes_accessed=2_000_000, transcendentals=0),
        name="lay_out_rows",
    )(block, column)


def hidden_kernel(member_ref, rows_ref, *refs):
    own, beside, out_ref = refs[:4], refs[4:8], refs[8]
    units = own[0].shape[1]
    width = rows_ref.shape[4]
    for kind in range(2):
        rows = [rows_ref[:, far, kind].reshape(-1, width) for far in range(2)]
        for core, pieces in enumerate((own, beside)):
            total = None
            for far in range(2):
                weight = jnp.concatenate(
                    [piece[kind, :, far * width : (far + 1) * width] for piece in pieces], axis=0
                )
                term = dot(weight, rows[far], 1, 1)
                total = term if total is None else total + term
            total = total.astype(BF16)
            for step in range(4):
                for at in range(4):
                    out_ref[at, member_ref[0] ^ step, kind, core] = total[step * units : (step + 1) * units]


def hidden_parts(member, rows, own, beside):
    units = own[0].shape[1]
    tokens = rows.shape[0] * rows.shape[3]
    return pl.pallas_call(
        hidden_kernel,
        out_shape=jax.ShapeDtypeStruct((4, 4, 2, 2, units, tokens), BF16),
        in_specs=[pl.BlockSpec(memory_space=pltpu.SMEM)] + [pl.BlockSpec(memory_space=pltpu.VMEM)] * 9,
        out_specs=pl.BlockSpec(memory_space=pltpu.VMEM),
        compiler_params=pltpu.CompilerParams(vmem_limit_bytes=VMEM_BYTES),
        cost_estimate=pl.CostEstimate(flops=604_000_000, bytes_accessed=6_700_000, transcendentals=0),
        name="hidden_parts",
    )(member, rows, *own, *beside)


def output_kernel(member_ref, parts_ref, *refs):
    own, beside, out_ref, pair_ref = refs[:4], refs[4:8], refs[8], refs[9]
    features = own[0].shape[2]
    count, unused, rows, unused = out_ref.shape
    step_of = features // 4
    units = [[], []]
    for core in range(2):
        for step in range(4):
            slot = member_ref[0] ^ step
            pre_act, act_grad = (
                sum(parts_ref[source, slot, kind, core].astype(F32) for source in range(4)) for kind in range(2)
            )
            values = (activate(pre_act).astype(BF16), gelu_slope(pre_act, act_grad).astype(BF16))
            for kind in range(2):
                units[kind].append(values[kind])
                if step < 2:
                    pair_ref[core, kind, 0, slot % 2] = values[kind]
    for result in range(2):
        left = jnp.concatenate(units[result], axis=0)
        for at in range(4):
            columns = slice(at * step_of, (at + 1) * step_of)
            weight = jnp.concatenate(
                [piece[1 - result, :, columns] for piece in (*own, *beside)], axis=0
            )
            total = dot(left, weight, 0, 0)
            out_ref[:, result, :, columns] = total.astype(BF16).reshape(count, rows, step_of)


def output_parts(member, parts, own, beside, count):
    features = own[0].shape[2]
    units, tokens = parts.shape[4:]
    return pl.pallas_call(
        output_kernel,
        out_shape=[
            jax.ShapeDtypeStruct((count, 2, tokens // count, features), BF16),
            jax.ShapeDtypeStruct((2, 2, 1, 2, units, tokens), BF16),
        ],
        in_specs=[pl.BlockSpec(memory_space=pltpu.SMEM)] + [pl.BlockSpec(memory_space=pltpu.VMEM)] * 9,
        out_specs=[pl.BlockSpec(memory_space=pltpu.VMEM)] * 2,
        compiler_params=pltpu.CompilerParams(vmem_limit_bytes=VMEM_BYTES),
        cost_estimate=pl.CostEstimate(flops=604_000_000, bytes_accessed=6_700_000, transcendentals=49_152),
        name="output_parts",
    )(member, parts, *own, *beside)


def local(tokens, up_proj, down_proj, out_grad):
    width = tokens.shape[1]
    units = down_proj.shape[0]
    member = lax.axis_index(GROUP).reshape(1).astype(jnp.int32)

    pieces = cut(member, up_proj.T, down_proj)
    own = [pieces[0]] + [partner(pieces[step], GROUP, 4, step) for step in range(1, 4)]
    first = other_core(after(pieces[0], *own[1:]))
    beside = [first] + [other_core(piece) for piece in own[1:]]

    both = after(jnp.concatenate([tokens, out_grad], axis=0), *pieces)
    column = spread(both, COLUMN, 8)
    sent, mine = lay_out(lax.axis_index(("z2", "z1")).reshape(1).astype(jnp.int32), column)
    plane = exchange(after(sent, *own), PLANE)

    lines = gather_ring(after(mine, first), "y", 4, 2)
    parts = hidden_parts(after(member, lines), plane, own, beside)
    arrived = exchange(parts, GROUP)
    flat = gather_ring(after(lines, parts), ("xh", "xp"), 4, 1).reshape(2, 128, width)

    partials, pair = output_parts(member, arrived, own, beside, 16)
    arrived = exchange(partials, PLANE)
    summed = jnp.sum(arrived.reshape(2, 2, 4, 2, 8, 2 * width).astype(F32), axis=(0, 2))
    summed = summed.astype(BF16).reshape(2, 2, 2, 4, 2, width)
    summed = summed.transpose(2, 4, 0, 1, 3, 5).reshape(8, 2, 4, width)
    ends = jnp.sum(exchange(summed, COLUMN).astype(F32), axis=0).astype(BF16)

    flat = jnp.concatenate([flat, other_core(flat)], axis=1)
    lines = gather_ring(pair, ("z2", "z1"), 4, 2)
    lines = after(lines, arrived).reshape(2, 2, 8 * units, 128)
    units_all = jnp.concatenate([lines[0], other_core(lines[1])], axis=2)
    down_grad = dot(units_all[0], flat[1], 1, 0).astype(BF16)
    up_grad = dot(flat[0], units_all[1], 0, 1).astype(BF16)
    return (ends[0], ends[1], up_grad, down_grad)


def solution(mesh):
    fine = Mesh(
        mesh.devices.reshape(2, 2, 2, 4, 2, 2, 2, 2),
        ("xh", "xp", "zh", "y", "c", "z2", "z1", "zp"),
    )
    owners = ("xh", "xp", "zh", "y", "c")
    features = ("z2", "z1", "zp")
    return jax.shard_map(
        local,
        mesh=fine,
        in_specs=(
            P(owners, features),
            P(None, owners + features),
            P(owners + features, None),
            P(owners, features),
        ),
        out_specs=(
            P(owners, features),
            P(owners, features),
            P(features, owners),
            P(owners, features),
        ),
        check_vma=False,
    )
```

```python
import jax
import jax.numpy as jnp
from jax import lax
from jax.experimental import pallas as pl
from jax.experimental.pallas import tpu as pltpu
from jax.sharding import Mesh, PartitionSpec as P

BF16 = jnp.bfloat16
F32 = jnp.float32
VMEM_BYTES = 60 * 1024 * 1024

PLANE = ("x", "y")
COLUMN = ("zh", "z2")
GROUP = ("m",)


def activate(values):
    return jax.nn.gelu(values, approximate=True)


def gelu_slope(pre_act, cotangent):
    unused, pullback = jax.vjp(activate, pre_act)
    return pullback(cotangent)[0]


def exchange(value, axes):
    return lax.all_to_all(value, axes, split_axis=0, concat_axis=0, tiled=True)


def spread(value, axes, count):
    return exchange(jnp.broadcast_to(value[None], (count,) + value.shape), axes)


def partner(value, axes, count, step):
    return lax.ppermute(value, axes, [(at, at ^ step) for at in range(count)])


def other_core(value):
    return partner(value, "c", 2, 1)


def gather_ring(value, axes, count, dim):
    here = lax.axis_index(axes)
    shape = list(value.shape)
    shape[dim] = count
    start = [0] * len(shape)
    whole = jnp.zeros(shape, value.dtype)
    blocks = [value] + [partner(value, axes, count, step) for step in range(1, count)]
    for step, block in enumerate(lax.optimization_barrier(blocks)):
        start[dim] = here ^ step
        whole = lax.dynamic_update_slice(whole, block, tuple(start))
    return whole


def after(value, *others):
    return lax.optimization_barrier((value,) + others)[0]


def dot(left, right, left_dim, right_dim):
    return lax.dot_general(
        left, right, (((left_dim,), (right_dim,)), ((), ())), preferred_element_type=F32
    )


def cut_kernel(place_ref, up_ref, down_ref, *refs):
    pieces, held_ref, in_sems, out_sems = refs[:7], refs[7], refs[8], refs[9]
    width = held_ref.shape[3] // 2
    arriving = {}
    for kind, source in enumerate((up_ref, down_ref)):
        for step in range(4):
            for far in range(2):
                column = pl.multiple_of((far * 4 + (place_ref[0] ^ step)) * width, width)
                arriving[kind, step, far] = pltpu.make_async_copy(
                    source.at[:, pl.ds(column, width)],
                    held_ref.at[step, kind, :, pl.ds(far * width, width)],
                    in_sems.at[kind * 8 + step * 2 + far],
                )
                arriving[kind, step, far].start()
    leaving = []
    for kind in range(2):
        for step in range(1, 4):
            for far in range(2):
                arriving[kind, step, far].wait()
            at = kind * 3 + step
            leaving.append(pltpu.make_async_copy(held_ref.at[step, kind], pieces[at], out_sems.at[at]))
            leaving[-1].start()
    for kind in range(2):
        for far in range(2):
            arriving[kind, 0, far].wait()
    leaving.append(pltpu.make_async_copy(held_ref.at[0], pieces[0], out_sems.at[0]))
    leaving[-1].start()
    for copy in leaving:
        copy.wait()


def cut(place, up_rows, down_rows):
    units, features = up_rows.shape
    pair = (2, units, features // 4)
    return pl.pallas_call(
        cut_kernel,
        out_shape=[jax.ShapeDtypeStruct(pair, BF16)] + [jax.ShapeDtypeStruct(pair[1:], BF16)] * 6,
        in_specs=[pl.BlockSpec(memory_space=pltpu.SMEM)] + [pl.BlockSpec(memory_space=pltpu.HBM)] * 2,
        out_specs=[pl.BlockSpec(memory_space=pltpu.HBM)] * 7,
        scratch_shapes=[
            pltpu.VMEM((4,) + pair, BF16),
            pltpu.SemaphoreType.DMA((16,)),
            pltpu.SemaphoreType.DMA((7,)),
        ],
        compiler_params=pltpu.CompilerParams(vmem_limit_bytes=VMEM_BYTES),
        cost_estimate=pl.CostEstimate(flops=0, bytes_accessed=16 * units * features, transcendentals=0),
        name="cut_weights",
    )(place, up_rows, down_rows)


def lay_out_kernel(column_ref, sent_ref):
    for far in range(2):
        ends = [column_ref[end * 2 + far].astype(F32) for end in range(2)]
        for array in range(2):
            rows = jnp.concatenate([end[array * 4 : array * 4 + 4] for end in ends], axis=0).astype(BF16)
            for at in range(sent_ref.shape[0]):
                sent_ref[at, far, array] = rows


def lay_out(column, count):
    unused, rows, width = column.shape
    return pl.pallas_call(
        lay_out_kernel,
        out_shape=jax.ShapeDtypeStruct((count, 2, 2, rows, width), BF16),
        in_specs=[pl.BlockSpec(memory_space=pltpu.VMEM)],
        out_specs=pl.BlockSpec(memory_space=pltpu.VMEM),
        compiler_params=pltpu.CompilerParams(vmem_limit_bytes=VMEM_BYTES),
        cost_estimate=pl.CostEstimate(flops=0, bytes_accessed=2_000_000, transcendentals=0),
        name="lay_out_rows",
    )(column)


def fetch(pieces, held_ref, sems):
    units = pieces[0].shape[1]
    copies = [[], []]
    for core in range(2):
        for at, piece in enumerate(pieces[core * 7 : core * 7 + 7]):
            if at == 0:
                target = held_ref.at[:, pl.ds(core * 4 * units, units), :]
            else:
                kind, step = (at - 1) // 3, (at - 1) % 3 + 1
                target = held_ref.at[kind, pl.ds((core * 4 + step) * units, units), :]
            copies[core].append(pltpu.make_async_copy(piece, target, sems.at[core * 7 + at]))
            copies[core][-1].start()
    return copies


def hidden_kernel(place_ref, rows_ref, *refs):
    pieces, (out_ref, mine_ref, held_ref, sems) = refs[:14], refs[14:]
    units = pieces[0].shape[1]
    width = rows_ref.shape[4]
    copies = fetch(pieces, held_ref, sems)
    for kind in range(2):
        mine_ref[kind] = rows_ref[:, place_ref[1], kind].reshape(-1, width)
    for core in range(2):
        for copy in copies[core]:
            copy.wait()
        for kind in range(2):
            total = None
            for far in range(2):
                weight = held_ref[kind, core * 4 * units : (core + 1) * 4 * units, far * width : (far + 1) * width]
                term = dot(weight, rows_ref[:, far, kind].reshape(-1, width), 1, 1)
                total = term if total is None else total + term
            total = total.astype(BF16)
            for step in range(4):
                for at in range(4):
                    out_ref[at, place_ref[0] ^ step, kind, core] = total[step * units : (step + 1) * units]


def hidden_parts(place, rows, own, beside):
    units, features = own[0].shape[1:]
    tokens = rows.shape[0] * rows.shape[3]
    return pl.pallas_call(
        hidden_kernel,
        out_shape=[
            jax.ShapeDtypeStruct((4, 4, 2, 2, units, tokens), BF16),
            jax.ShapeDtypeStruct((2, tokens, features // 2), BF16),
        ],
        in_specs=[pl.BlockSpec(memory_space=pltpu.SMEM), pl.BlockSpec(memory_space=pltpu.VMEM)]
        + [pl.BlockSpec(memory_space=pltpu.HBM)] * 14,
        out_specs=[pl.BlockSpec(memory_space=pltpu.VMEM)] * 2,
        scratch_shapes=[pltpu.VMEM((2, 8 * units, features), BF16), pltpu.SemaphoreType.DMA((14,))],
        compiler_params=pltpu.CompilerParams(vmem_limit_bytes=VMEM_BYTES),
        cost_estimate=pl.CostEstimate(flops=604_000_000, bytes_accessed=6_700_000, transcendentals=0),
        name="hidden_parts",
    )(place, rows, *own, *beside)


def output_kernel(place_ref, parts_ref, *refs):
    pieces, (out_ref, quad_ref, held_ref, sems) = refs[:14], refs[14:]
    features = pieces[0].shape[2]
    count, unused, rows, unused = out_ref.shape
    step_of = features // 4
    copies = fetch(pieces, held_ref, sems)
    units = [[], []]
    for core in range(2):
        for step in range(4):
            slot = place_ref[0] ^ step
            pre_act, act_grad = (
                sum(parts_ref[source, slot, kind, core].astype(F32) for source in range(4)) for kind in range(2)
            )
            values = (activate(pre_act).astype(BF16), gelu_slope(pre_act, act_grad).astype(BF16))
            for kind in range(2):
                units[kind].append(values[kind])
                quad_ref[core, kind, 0, slot] = values[kind]
    for copy in copies[0] + copies[1]:
        copy.wait()
    for result in range(2):
        left = jnp.concatenate(units[result], axis=0)
        for at in range(4):
            columns = slice(at * step_of, (at + 1) * step_of)
            total = dot(left, held_ref[1 - result, :, columns], 0, 0)
            out_ref[:, result, :, columns] = total.astype(BF16).reshape(count, rows, step_of)


def output_parts(place, parts, own, beside, count):
    features = own[0].shape[2]
    units, tokens = parts.shape[4:]
    return pl.pallas_call(
        output_kernel,
        out_shape=[
            jax.ShapeDtypeStruct((count, 2, tokens // count, features), BF16),
            jax.ShapeDtypeStruct((2, 2, 1, 4, units, tokens), BF16),
        ],
        in_specs=[pl.BlockSpec(memory_space=pltpu.SMEM), pl.BlockSpec(memory_space=pltpu.VMEM)]
        + [pl.BlockSpec(memory_space=pltpu.HBM)] * 14,
        out_specs=[pl.BlockSpec(memory_space=pltpu.VMEM)] * 2,
        scratch_shapes=[pltpu.VMEM((2, 8 * units, features), BF16), pltpu.SemaphoreType.DMA((14,))],
        compiler_params=pltpu.CompilerParams(vmem_limit_bytes=VMEM_BYTES),
        cost_estimate=pl.CostEstimate(flops=604_000_000, bytes_accessed=6_700_000, transcendentals=49_152),
        name="output_parts",
    )(place, parts, *own, *beside)


def local(tokens, up_proj, down_proj, out_grad):
    width = tokens.shape[1]
    units = down_proj.shape[0]
    place = jnp.stack([lax.axis_index("m"), lax.axis_index("z2")]).astype(jnp.int32)

    pieces = cut(place, up_proj.T, down_proj)
    first = other_core(pieces[0])
    own = [pieces[0]] + [partner(pieces[at], GROUP, 4, (at - 1) % 3 + 1) for at in range(1, 7)]
    beside = [first] + [other_core(piece) for piece in own[1:]]

    both = after(jnp.concatenate([tokens, out_grad], axis=0), first)
    column = spread(both, COLUMN, 4)
    sent = lay_out(column, 16)
    plane = exchange(after(sent, *own[1:4]), PLANE)

    parts, mine = hidden_parts(place, plane, own, beside)
    arrived = exchange(parts, GROUP)

    partials, quad = output_parts(place, arrived, own, beside, 16)
    arrived = exchange(partials, PLANE)
    summed = jnp.sum(arrived.reshape(16, 2, 2, 4, 2, width).astype(F32), axis=0)
    summed = summed.transpose(1, 3, 0, 2, 4).reshape(4, 2, 4, width)
    ends = jnp.sum(exchange(summed, COLUMN), axis=0).astype(BF16)

    flat = jnp.concatenate([mine, other_core(mine)], axis=1)
    lines = gather_ring(quad, "z2", 2, 2)
    lines = after(lines, arrived).reshape(2, 2, 8 * units, 128)
    units_all = jnp.concatenate([lines[0], other_core(lines[1])], axis=2)
    down_grad = dot(units_all[0], flat[1], 1, 0).astype(BF16)
    up_grad = dot(flat[0], units_all[1], 0, 1).astype(BF16)
    return (ends[0], ends[1], up_grad, down_grad)


def solution(mesh):
    fine = Mesh(mesh.devices.reshape(4, 2, 4, 2, 2, 4), ("x", "zh", "y", "c", "z2", "m"))
    owners = ("x", "zh", "y", "c")
    features = ("z2", "m")
    return jax.shard_map(
        local,
        mesh=fine,
        in_specs=(
            P(owners, features),
            P(None, owners + features),
            P(owners + features, None),
            P(owners, features),
        ),
        out_specs=(
            P(owners, features),
            P(owners, features),
            P(features, owners),
            P(owners, features),
        ),
        check_vma=False,
    )
```

```python
import jax
import jax.numpy as jnp
from jax import lax
from jax.experimental import pallas as pl
from jax.experimental.pallas import tpu as pltpu
from jax.sharding import Mesh, PartitionSpec as P

BF16 = jnp.bfloat16
F32 = jnp.float32
VMEM_BYTES = 20 * 1024 * 1024

PLANE = ("xh", "xp", "y")
COLUMN = ("zh", "z2", "z1")
GROUP = ("xp", "zp")


def activate(values):
    return jax.nn.gelu(values, approximate=True)


def gelu_slope(pre_act, cotangent):
    unused, pullback = jax.vjp(activate, pre_act)
    return pullback(cotangent)[0]


def exchange(value, axes):
    return lax.all_to_all(value, axes, split_axis=0, concat_axis=0, tiled=True)


def spread(value, axes, count):
    return exchange(jnp.broadcast_to(value[None], (count,) + value.shape), axes)


def partner(value, axes, count, step):
    return lax.ppermute(value, axes, [(at, at ^ step) for at in range(count)])


def other_core(value):
    return partner(value, "c", 2, 1)


def gather_ring(value, axes, count, dim, *others):
    here = lax.axis_index(axes)
    shape = list(value.shape)
    shape[dim] = count
    start = [0] * len(shape)
    whole = jnp.zeros(shape, value.dtype)
    blocks = [value] + [partner(value, axes, count, step) for step in range(1, count)]
    for step, block in enumerate(lax.optimization_barrier(blocks + list(others))[:count]):
        start[dim] = here ^ step
        whole = lax.dynamic_update_slice(whole, block, tuple(start))
    return whole


def after(value, *others):
    return lax.optimization_barrier((value,) + others)[0]


def dot(left, right, left_dim, right_dim):
    return lax.dot_general(
        left, right, (((left_dim,), (right_dim,)), ((), ())), preferred_element_type=F32
    )


def cut_kernel(member_ref, up_ref, down_ref, *pieces):
    width = pieces[0].shape[2] // 2
    for step in range(4):
        for kind, source in enumerate((up_ref, down_ref)):
            for far in range(2):
                column = pl.multiple_of((far * 4 + (member_ref[0] ^ step)) * width, width)
                pieces[step][kind, :, far * width : (far + 1) * width] = source[:, pl.ds(column, width)]


def cut(member, up_rows, down_rows):
    units, features = up_rows.shape
    piece = jax.ShapeDtypeStruct((2, units, features // 4), BF16)
    return pl.pallas_call(
        cut_kernel,
        out_shape=[piece] * 4,
        in_specs=[pl.BlockSpec(memory_space=pltpu.SMEM)] + [pl.BlockSpec(memory_space=pltpu.VMEM)] * 2,
        out_specs=[pl.BlockSpec(memory_space=pltpu.VMEM)] * 4,
        compiler_params=pltpu.CompilerParams(vmem_limit_bytes=VMEM_BYTES),
        cost_estimate=pl.CostEstimate(flops=0, bytes_accessed=8 * units * features, transcendentals=0),
        name="cut_weights",
    )(member, up_rows, down_rows)


def lay_out_kernel(block_ref, column_ref, sent_ref, mine_ref):
    for far in range(2):
        for near in range(2):
            ends = [column_ref[end * 4 + far * 2 + near].astype(F32) for end in range(2)]
            for array in range(2):
                rows = jnp.concatenate([end[array * 4 : array * 4 + 4] for end in ends], axis=0).astype(BF16)
                for half in range(2):
                    for line in range(4):
                        sent_ref[half * 8 + near * 4 + line, far, array] = rows
    ends = [column_ref[end * 4 + block_ref[0]].astype(F32) for end in range(2)]
    for array in range(2):
        rows = jnp.concatenate([end[array * 4 : array * 4 + 4] for end in ends], axis=0)
        mine_ref[array, 0, 0] = rows.astype(BF16)


def lay_out(block, column):
    unused, rows, width = column.shape
    return pl.pallas_call(
        lay_out_kernel,
        out_shape=[
            jax.ShapeDtypeStruct((16, 2, 2, rows, width), BF16),
            jax.ShapeDtypeStruct((2, 1, 1, rows, width), BF16),
        ],
        in_specs=[pl.BlockSpec(memory_space=pltpu.SMEM), pl.BlockSpec(memory_space=pltpu.VMEM)],
        out_specs=[pl.BlockSpec(memory_space=pltpu.VMEM)] * 2,
        compiler_params=pltpu.CompilerParams(vmem_limit_bytes=VMEM_BYTES),
        cost_estimate=pl.CostEstimate(flops=0, bytes_accessed=2_000_000, transcendentals=0),
        name="lay_out_rows",
    )(block, column)


def hidden_kernel(member_ref, rows_ref, *refs):
    own, beside, out_ref = refs[:4], refs[4:8], refs[8]
    units = own[0].shape[1]
    width = rows_ref.shape[4]
    for kind in range(2):
        rows = [rows_ref[:, far, kind].reshape(-1, width) for far in range(2)]
        for core, pieces in enumerate((own, beside)):
            total = None
            for far in range(2):
                weight = jnp.concatenate(
                    [piece[kind, :, far * width : (far + 1) * width] for piece in pieces], axis=0
                )
                term = dot(weight, rows[far], 1, 1)
                total = term if total is None else total + term
            sends = [(kind, total.astype(BF16))]
            if kind == 0:
                sends.append((2, (total - sends[0][1].astype(F32)).astype(BF16)))
            for row, value in sends:
                for step in range(4):
                    for at in range(4):
                        out_ref[at, member_ref[0] ^ step, row, core] = value[step * units : (step + 1) * units]


def hidden_parts(member, rows, own, beside):
    units = own[0].shape[1]
    tokens = rows.shape[0] * rows.shape[3]
    return pl.pallas_call(
        hidden_kernel,
        out_shape=jax.ShapeDtypeStruct((4, 4, 3, 2, units, tokens), BF16),
        in_specs=[pl.BlockSpec(memory_space=pltpu.SMEM)] + [pl.BlockSpec(memory_space=pltpu.VMEM)] * 9,
        out_specs=pl.BlockSpec(memory_space=pltpu.VMEM),
        compiler_params=pltpu.CompilerParams(vmem_limit_bytes=VMEM_BYTES),
        cost_estimate=pl.CostEstimate(flops=604_000_000, bytes_accessed=6_700_000, transcendentals=0),
        name="hidden_parts",
    )(member, rows, *own, *beside)


def output_kernel(member_ref, parts_ref, *refs):
    own, beside, out_ref, pair_ref = refs[:4], refs[4:8], refs[8], refs[9]
    features = own[0].shape[2]
    count, unused, rows, unused = out_ref.shape
    step_of = features // 4
    units = [[], []]
    for core in range(2):
        for step in range(4):
            slot = member_ref[0] ^ step
            value, act_grad, rest = (
                sum(parts_ref[source, slot, row, core].astype(F32) for source in range(4)) for row in range(3)
            )
            pre_act = value + rest
            values = (activate(pre_act).astype(BF16), gelu_slope(pre_act, act_grad).astype(BF16))
            for kind in range(2):
                units[kind].append(values[kind])
                if step < 2:
                    pair_ref[core, kind, 0, slot % 2] = values[kind]
    for result in range(2):
        left = jnp.concatenate(units[result], axis=0)
        for at in range(4):
            columns = slice(at * step_of, (at + 1) * step_of)
            weight = jnp.concatenate(
                [piece[1 - result, :, columns] for piece in (*own, *beside)], axis=0
            )
            total = dot(left, weight, 0, 0)
            out_ref[:, result, :, columns] = total.astype(BF16).reshape(count, rows, step_of)


def output_parts(member, parts, own, beside, count):
    features = own[0].shape[2]
    units, tokens = parts.shape[4:]
    return pl.pallas_call(
        output_kernel,
        out_shape=[
            jax.ShapeDtypeStruct((count, 2, tokens // count, features), BF16),
            jax.ShapeDtypeStruct((2, 2, 1, 2, units, tokens), BF16),
        ],
        in_specs=[pl.BlockSpec(memory_space=pltpu.SMEM)] + [pl.BlockSpec(memory_space=pltpu.VMEM)] * 9,
        out_specs=[pl.BlockSpec(memory_space=pltpu.VMEM)] * 2,
        compiler_params=pltpu.CompilerParams(vmem_limit_bytes=VMEM_BYTES),
        cost_estimate=pl.CostEstimate(flops=604_000_000, bytes_accessed=6_700_000, transcendentals=49_152),
        name="output_parts",
    )(member, parts, *own, *beside)


def local(tokens, up_proj, down_proj, out_grad):
    width = tokens.shape[1]
    units = down_proj.shape[0]
    member = lax.axis_index(GROUP).reshape(1).astype(jnp.int32)

    pieces = cut(member, up_proj.T, down_proj)
    own = [pieces[0]] + [partner(pieces[step], GROUP, 4, step) for step in range(1, 4)]
    beside = [other_core(piece) for piece in own]

    both = after(jnp.concatenate([tokens, out_grad], axis=0), beside[0])
    column = spread(both, COLUMN, 8)
    sent, mine = lay_out(lax.axis_index(("z2", "z1")).reshape(1).astype(jnp.int32), after(column, *beside))
    plane = exchange(sent, PLANE)

    lines = gather_ring(after(mine, sent), "y", 4, 2)
    parts = hidden_parts(after(member, lines), plane, own, beside)
    arrived = exchange(parts, GROUP)
    flat = gather_ring(after(lines, parts), ("xh", "xp"), 4, 1).reshape(2, 128, width)

    partials, pair = output_parts(after(member, flat), arrived, own, beside, 16)
    arrived = exchange(partials, PLANE)
    summed = jnp.sum(arrived.reshape(2, 2, 4, 2, 8, 2 * width).astype(F32), axis=(0, 2))
    summed = summed.astype(BF16).reshape(2, 2, 2, 4, 2, width)
    summed = summed.transpose(2, 4, 0, 1, 3, 5).reshape(8, 2, 4, width)
    ends = jnp.sum(exchange(summed, COLUMN).astype(F32), axis=0).astype(BF16)

    flat = jnp.concatenate([flat, other_core(flat)], axis=1)
    lines = gather_ring(pair, "z2", 2, 2)[:, :, :, None]
    lines = gather_ring(lines, "z1", 2, 3, arrived)
    lines = lines.reshape(2, 2, 8 * units, 128)
    units_all = jnp.concatenate([lines[0], other_core(lines[1])], axis=2)
    down_grad = dot(units_all[0], flat[1], 1, 0).astype(BF16)
    up_grad = dot(flat[0], units_all[1], 0, 1).astype(BF16)
    return (ends[0], ends[1], up_grad, down_grad)


def solution(mesh):
    fine = Mesh(
        mesh.devices.reshape(2, 2, 2, 4, 2, 2, 2, 2),
        ("xh", "xp", "zh", "y", "c", "z2", "z1", "zp"),
    )
    owners = ("xh", "xp", "zh", "y", "c")
    features = ("z2", "z1", "zp")
    return jax.shard_map(
        local,
        mesh=fine,
        in_specs=(
            P(owners, features),
            P(None, owners + features),
            P(owners + features, None),
            P(owners, features),
        ),
        out_specs=(
            P(owners, features),
            P(owners, features),
            P(features, owners),
            P(owners, features),
        ),
        check_vma=False,
    )
```

```python
import jax
import jax.numpy as jnp
from jax import lax
from jax.experimental import pallas as pl
from jax.experimental.pallas import tpu as pltpu
from jax.sharding import Mesh, PartitionSpec as P

BF16 = jnp.bfloat16
F32 = jnp.float32
VMEM_BYTES = 20 * 1024 * 1024

PLANE = ("xh", "xp", "y")
COLUMN = ("zh", "z2", "z1")
GROUP = ("xp", "zp")


def activate(values):
    return jax.nn.gelu(values, approximate=True)


def gelu_slope(pre_act, cotangent):
    unused, pullback = jax.vjp(activate, pre_act)
    return pullback(cotangent)[0]


def exchange(value, axes):
    return lax.all_to_all(value, axes, split_axis=0, concat_axis=0, tiled=True)


def spread(value, axes, count):
    return exchange(jnp.broadcast_to(value[None], (count,) + value.shape), axes)


def partner(value, axes, count, step):
    return lax.ppermute(value, axes, [(at, at ^ step) for at in range(count)])


def other_core(value):
    return partner(value, "c", 2, 1)


def gather_ring(value, axes, count, dim, *others):
    here = lax.axis_index(axes)
    shape = list(value.shape)
    shape[dim] = count
    start = [0] * len(shape)
    whole = jnp.zeros(shape, value.dtype)
    blocks = [value] + [partner(value, axes, count, step) for step in range(1, count)]
    for step, block in enumerate(lax.optimization_barrier(blocks + list(others))[:count]):
        start[dim] = here ^ step
        whole = lax.dynamic_update_slice(whole, block, tuple(start))
    return whole


def after(value, *others):
    return lax.optimization_barrier((value,) + others)[0]


def dot(left, right, left_dim, right_dim):
    return lax.dot_general(
        left, right, (((left_dim,), (right_dim,)), ((), ())), preferred_element_type=F32
    )


def cut_kernel(member_ref, up_ref, down_ref, *pieces):
    width = pieces[0].shape[2] // 2
    for step in range(4):
        for kind, source in enumerate((up_ref, down_ref)):
            for far in range(2):
                column = pl.multiple_of((far * 4 + (member_ref[0] ^ step)) * width, width)
                pieces[step][kind, :, far * width : (far + 1) * width] = source[:, pl.ds(column, width)]


def cut(member, up_rows, down_rows):
    units, features = up_rows.shape
    piece = jax.ShapeDtypeStruct((2, units, features // 4), BF16)
    return pl.pallas_call(
        cut_kernel,
        out_shape=[piece] * 4,
        in_specs=[pl.BlockSpec(memory_space=pltpu.SMEM)] + [pl.BlockSpec(memory_space=pltpu.VMEM)] * 2,
        out_specs=[pl.BlockSpec(memory_space=pltpu.VMEM)] * 4,
        compiler_params=pltpu.CompilerParams(vmem_limit_bytes=VMEM_BYTES),
        cost_estimate=pl.CostEstimate(flops=0, bytes_accessed=8 * units * features, transcendentals=0),
        name="cut_weights",
    )(member, up_rows, down_rows)


def lay_out_kernel(block_ref, column_ref, sent_ref):
    def rows_of(at, array):
        ends = [column_ref[end * 4 + at, array * 4 : array * 4 + 4].astype(F32) for end in range(2)]
        return jnp.concatenate(ends, axis=0).astype(BF16)

    for array in range(2):
        own = rows_of(block_ref[0], array)
        for near in range(2):
            blocks = [rows_of(far * 2 + near, array) for far in range(2)] + [own]
            for half in range(2):
                for line in range(4):
                    for far in range(3):
                        sent_ref[half * 8 + near * 4 + line, far, array] = blocks[far]


def lay_out(block, column):
    unused, rows, width = column.shape
    return pl.pallas_call(
        lay_out_kernel,
        out_shape=jax.ShapeDtypeStruct((16, 3, 2, rows, width), BF16),
        in_specs=[pl.BlockSpec(memory_space=pltpu.SMEM), pl.BlockSpec(memory_space=pltpu.VMEM)],
        out_specs=pl.BlockSpec(memory_space=pltpu.VMEM),
        compiler_params=pltpu.CompilerParams(vmem_limit_bytes=VMEM_BYTES),
        cost_estimate=pl.CostEstimate(flops=0, bytes_accessed=2_800_000, transcendentals=0),
        name="lay_out_rows",
    )(block, column)


def hidden_kernel(member_ref, rows_ref, *refs):
    own, beside, out_ref, mine_ref = refs[:4], refs[4:8], refs[8], refs[9]
    units = own[0].shape[1]
    width = rows_ref.shape[4]
    for kind in range(2):
        rows = [rows_ref[:, far, kind].reshape(-1, width) for far in range(3)]
        mine_ref[kind] = rows[2]
        for core, pieces in enumerate((own, beside)):
            total = None
            for far in range(2):
                weight = jnp.concatenate(
                    [piece[kind, :, far * width : (far + 1) * width] for piece in pieces], axis=0
                )
                term = dot(weight, rows[far], 1, 1)
                total = term if total is None else total + term
            sends = [(kind, total.astype(BF16))]
            if kind == 0:
                sends.append((2, (total - sends[0][1].astype(F32)).astype(BF16)))
            for row, value in sends:
                for step in range(4):
                    for at in range(4):
                        out_ref[at, member_ref[0] ^ step, row, core] = value[step * units : (step + 1) * units]


def hidden_parts(member, rows, own, beside):
    units = own[0].shape[1]
    tokens = rows.shape[0] * rows.shape[3]
    return pl.pallas_call(
        hidden_kernel,
        out_shape=[
            jax.ShapeDtypeStruct((4, 4, 3, 2, units, tokens), BF16),
            jax.ShapeDtypeStruct((2, tokens, rows.shape[4]), BF16),
        ],
        in_specs=[pl.BlockSpec(memory_space=pltpu.SMEM)] + [pl.BlockSpec(memory_space=pltpu.VMEM)] * 9,
        out_specs=[pl.BlockSpec(memory_space=pltpu.VMEM)] * 2,
        compiler_params=pltpu.CompilerParams(vmem_limit_bytes=VMEM_BYTES),
        cost_estimate=pl.CostEstimate(flops=604_000_000, bytes_accessed=6_700_000, transcendentals=0),
        name="hidden_parts",
    )(member, rows, *own, *beside)


def output_kernel(member_ref, parts_ref, *refs):
    own, beside, out_ref, pair_ref = refs[:4], refs[4:8], refs[8], refs[9]
    features = own[0].shape[2]
    count, unused, rows, unused = out_ref.shape
    step_of = features // 4
    units = [[], []]
    for core in range(2):
        for step in range(4):
            slot = member_ref[0] ^ step
            value, act_grad, rest = (
                sum(parts_ref[source, slot, row, core].astype(F32) for source in range(4)) for row in range(3)
            )
            pre_act = value + rest
            values = (activate(pre_act).astype(BF16), gelu_slope(pre_act, act_grad).astype(BF16))
            for kind in range(2):
                units[kind].append(values[kind])
                if step < 2:
                    pair_ref[core, kind, 0, slot % 2] = values[kind]
    for result in range(2):
        left = jnp.concatenate(units[result], axis=0)
        for at in range(4):
            columns = slice(at * step_of, (at + 1) * step_of)
            weight = jnp.concatenate(
                [piece[1 - result, :, columns] for piece in (*own, *beside)], axis=0
            )
            total = dot(left, weight, 0, 0)
            out_ref[:, result, :, columns] = total.astype(BF16).reshape(count, rows, step_of)


def output_parts(member, parts, own, beside, count):
    features = own[0].shape[2]
    units, tokens = parts.shape[4:]
    return pl.pallas_call(
        output_kernel,
        out_shape=[
            jax.ShapeDtypeStruct((count, 2, tokens // count, features), BF16),
            jax.ShapeDtypeStruct((2, 2, 1, 2, units, tokens), BF16),
        ],
        in_specs=[pl.BlockSpec(memory_space=pltpu.SMEM)] + [pl.BlockSpec(memory_space=pltpu.VMEM)] * 9,
        out_specs=[pl.BlockSpec(memory_space=pltpu.VMEM)] * 2,
        compiler_params=pltpu.CompilerParams(vmem_limit_bytes=VMEM_BYTES),
        cost_estimate=pl.CostEstimate(flops=604_000_000, bytes_accessed=6_700_000, transcendentals=49_152),
        name="output_parts",
    )(member, parts, *own, *beside)


def local(tokens, up_proj, down_proj, out_grad):
    width = tokens.shape[1]
    units = down_proj.shape[0]
    member = lax.axis_index(GROUP).reshape(1).astype(jnp.int32)

    pieces = cut(member, up_proj.T, down_proj)
    own = [pieces[0]] + [partner(pieces[step], GROUP, 4, step) for step in range(1, 4)]
    beside = [other_core(pieces[0])]
    waits = own[1:]
    for piece in own[1:]:
        beside.append(other_core(after(piece, *waits)))
        waits = beside[-1:]

    both = jnp.concatenate([tokens, out_grad], axis=0)
    column = spread(both, COLUMN, 8)
    block = lax.axis_index(("z2", "z1")).reshape(1).astype(jnp.int32)
    sent = lay_out(block, after(column, beside[0]))
    plane = exchange(sent, PLANE)

    parts, mine = hidden_parts(member, plane, own, beside)
    arrived = exchange(parts, GROUP)

    partials, pair = output_parts(member, arrived, own, beside, 16)
    arrived = exchange(partials, PLANE)
    summed = jnp.sum(arrived.reshape(2, 2, 4, 2, 8, 2 * width).astype(F32), axis=(0, 2))
    summed = summed.astype(BF16).reshape(2, 2, 2, 4, 2, width)
    summed = summed.transpose(2, 4, 0, 1, 3, 5).reshape(8, 2, 4, width)
    ends = jnp.sum(exchange(summed, COLUMN).astype(F32), axis=0).astype(BF16)

    flat = jnp.concatenate([mine, other_core(mine)], axis=1)
    lines = gather_ring(pair, ("z2", "z1"), 4, 2, arrived)
    lines = lines.reshape(2, 2, 8 * units, 128)
    units_all = jnp.concatenate([lines[0], other_core(lines[1])], axis=2)
    down_grad = dot(units_all[0], flat[1], 1, 0).astype(BF16)
    up_grad = dot(flat[0], units_all[1], 0, 1).astype(BF16)
    return (ends[0], ends[1], up_grad, down_grad)


def solution(mesh):
    fine = Mesh(
        mesh.devices.reshape(2, 2, 2, 4, 2, 2, 2, 2),
        ("xh", "xp", "zh", "y", "c", "z2", "z1", "zp"),
    )
    owners = ("xh", "xp", "zh", "y", "c")
    features = ("z2", "z1", "zp")
    return jax.shard_map(
        local,
        mesh=fine,
        in_specs=(
            P(owners, features),
            P(None, owners + features),
            P(owners + features, None),
            P(owners, features),
        ),
        out_specs=(
            P(owners, features),
            P(owners, features),
            P(features, owners),
            P(owners, features),
        ),
        check_vma=False,
    )
```

```python
import jax
import jax.numpy as jnp
from jax import lax
from jax.experimental import pallas as pl
from jax.experimental.pallas import tpu as pltpu
from jax.sharding import Mesh, PartitionSpec as P

BF16 = jnp.bfloat16
F32 = jnp.float32
VMEM_BYTES = 20 * 1024 * 1024

PLANE = ("xh", "xp", "y")
COLUMN = ("zh", "z2", "z1")
GROUP = ("xp", "zp")


def activate(values):
    return jax.nn.gelu(values, approximate=True)


def gelu_slope(pre_act, cotangent):
    unused, pullback = jax.vjp(activate, pre_act)
    return pullback(cotangent)[0]


def exchange(value, axes):
    return lax.all_to_all(value, axes, split_axis=0, concat_axis=0, tiled=True)


def spread(value, axes, count):
    return exchange(jnp.broadcast_to(value[None], (count,) + value.shape), axes)


def partner(value, axes, count, step):
    return lax.ppermute(value, axes, [(at, at ^ step) for at in range(count)])


def other_core(value):
    return partner(value, "c", 2, 1)


def blocks_of(value, axes, count):
    return [value] + [partner(value, axes, count, step) for step in range(1, count)]


def in_order(blocks, axes, dim, *others):
    count, here = len(blocks), lax.axis_index(axes)
    shape = list(blocks[0].shape)
    shape[dim] = count
    start = [0] * len(shape)
    whole = jnp.zeros(shape, blocks[0].dtype)
    for step, block in enumerate(lax.optimization_barrier(list(blocks) + list(others))[:count]):
        start[dim] = here ^ step
        whole = lax.dynamic_update_slice(whole, block, tuple(start))
    return whole


def after(value, *others):
    return lax.optimization_barrier((value,) + others)[0]


def dot(left, right, left_dim, right_dim):
    return lax.dot_general(
        left, right, (((left_dim,), (right_dim,)), ((), ())), preferred_element_type=F32
    )


def cut_kernel(member_ref, up_ref, down_ref, *pieces):
    width = pieces[0].shape[2] // 2
    for step in range(4):
        for kind, source in enumerate((up_ref, down_ref)):
            for far in range(2):
                column = pl.multiple_of((far * 4 + (member_ref[0] ^ step)) * width, width)
                pieces[step][kind, :, far * width : (far + 1) * width] = source[:, pl.ds(column, width)]


def cut(member, up_rows, down_rows):
    units, features = up_rows.shape
    piece = jax.ShapeDtypeStruct((2, units, features // 4), BF16)
    return pl.pallas_call(
        cut_kernel,
        out_shape=[piece] * 4,
        in_specs=[pl.BlockSpec(memory_space=pltpu.SMEM)] + [pl.BlockSpec(memory_space=pltpu.VMEM)] * 2,
        out_specs=[pl.BlockSpec(memory_space=pltpu.VMEM)] * 4,
        compiler_params=pltpu.CompilerParams(vmem_limit_bytes=VMEM_BYTES),
        cost_estimate=pl.CostEstimate(flops=0, bytes_accessed=8 * units * features, transcendentals=0),
        name="cut_weights",
    )(member, up_rows, down_rows)


def lay_out_kernel(block_ref, column_ref, sent_ref, mine_ref):
    for far in range(2):
        for near in range(2):
            ends = [column_ref[end * 4 + far * 2 + near].astype(F32) for end in range(2)]
            for array in range(2):
                rows = jnp.concatenate([end[array * 4 : array * 4 + 4] for end in ends], axis=0).astype(BF16)
                for half in range(2):
                    for line in range(4):
                        sent_ref[half * 8 + near * 4 + line, far, array] = rows
    ends = [column_ref[end * 4 + block_ref[0]].astype(F32) for end in range(2)]
    for array in range(2):
        rows = jnp.concatenate([end[array * 4 : array * 4 + 4] for end in ends], axis=0)
        mine_ref[array, 0, 0] = rows.astype(BF16)


def lay_out(block, column):
    unused, rows, width = column.shape
    return pl.pallas_call(
        lay_out_kernel,
        out_shape=[
            jax.ShapeDtypeStruct((16, 2, 2, rows, width), BF16),
            jax.ShapeDtypeStruct((2, 1, 1, rows, width), BF16),
        ],
        in_specs=[pl.BlockSpec(memory_space=pltpu.SMEM), pl.BlockSpec(memory_space=pltpu.VMEM)],
        out_specs=[pl.BlockSpec(memory_space=pltpu.VMEM)] * 2,
        compiler_params=pltpu.CompilerParams(vmem_limit_bytes=VMEM_BYTES),
        cost_estimate=pl.CostEstimate(flops=0, bytes_accessed=2_000_000, transcendentals=0),
        name="lay_out_rows",
    )(block, column)


def hidden_kernel(member_ref, rows_ref, *refs):
    own, beside, out_ref = refs[:4], refs[4:8], refs[8]
    units = own[0].shape[1]
    width = rows_ref.shape[4]
    for kind in range(2):
        rows = [rows_ref[:, far, kind].reshape(-1, width) for far in range(2)]
        for core, pieces in enumerate((own, beside)):
            total = None
            for far in range(2):
                weight = jnp.concatenate(
                    [piece[kind, :, far * width : (far + 1) * width] for piece in pieces], axis=0
                )
                term = dot(weight, rows[far], 1, 1)
                total = term if total is None else total + term
            sends = [(kind, total.astype(BF16))]
            if kind == 0:
                sends.append((2, (total - sends[0][1].astype(F32)).astype(BF16)))
            for row, value in sends:
                for step in range(4):
                    for at in range(4):
                        out_ref[at, member_ref[0] ^ step, row, core] = value[step * units : (step + 1) * units]


def hidden_parts(member, rows, own, beside):
    units = own[0].shape[1]
    tokens = rows.shape[0] * rows.shape[3]
    return pl.pallas_call(
        hidden_kernel,
        out_shape=jax.ShapeDtypeStruct((4, 4, 3, 2, units, tokens), BF16),
        in_specs=[pl.BlockSpec(memory_space=pltpu.SMEM)] + [pl.BlockSpec(memory_space=pltpu.VMEM)] * 9,
        out_specs=pl.BlockSpec(memory_space=pltpu.VMEM),
        compiler_params=pltpu.CompilerParams(vmem_limit_bytes=VMEM_BYTES),
        cost_estimate=pl.CostEstimate(flops=604_000_000, bytes_accessed=6_700_000, transcendentals=0),
        name="hidden_parts",
    )(member, rows, *own, *beside)


def output_kernel(member_ref, parts_ref, *refs):
    own, beside, out_ref, pair_ref = refs[:4], refs[4:8], refs[8], refs[9]
    features = own[0].shape[2]
    count, unused, rows, unused = out_ref.shape
    step_of = features // 4
    units = [[], []]
    for core in range(2):
        for step in range(4):
            slot = member_ref[0] ^ step
            value, act_grad, rest = (
                sum(parts_ref[source, slot, row, core].astype(F32) for source in range(4)) for row in range(3)
            )
            pre_act = value + rest
            values = (activate(pre_act).astype(BF16), gelu_slope(pre_act, act_grad).astype(BF16))
            for kind in range(2):
                units[kind].append(values[kind])
                if step < 2:
                    pair_ref[core, kind, 0, slot % 2] = values[kind]
    for result in range(2):
        left = jnp.concatenate(units[result], axis=0)
        for at in range(4):
            columns = slice(at * step_of, (at + 1) * step_of)
            weight = jnp.concatenate(
                [piece[1 - result, :, columns] for piece in (*own, *beside)], axis=0
            )
            total = dot(left, weight, 0, 0)
            out_ref[:, result, :, columns] = total.astype(BF16).reshape(count, rows, step_of)


def output_parts(member, parts, own, beside, count):
    features = own[0].shape[2]
    units, tokens = parts.shape[4:]
    return pl.pallas_call(
        output_kernel,
        out_shape=[
            jax.ShapeDtypeStruct((count, 2, tokens // count, features), BF16),
            jax.ShapeDtypeStruct((2, 2, 1, 2, units, tokens), BF16),
        ],
        in_specs=[pl.BlockSpec(memory_space=pltpu.SMEM)] + [pl.BlockSpec(memory_space=pltpu.VMEM)] * 9,
        out_specs=[pl.BlockSpec(memory_space=pltpu.VMEM)] * 2,
        compiler_params=pltpu.CompilerParams(vmem_limit_bytes=VMEM_BYTES),
        cost_estimate=pl.CostEstimate(flops=604_000_000, bytes_accessed=6_700_000, transcendentals=49_152),
        name="output_parts",
    )(member, parts, *own, *beside)


def sum_kernel(arrived_ref, out_ref):
    width = out_ref.shape[3]
    for near in range(2):
        for array in range(2):
            total = None
            for half in range(2):
                for line in range(4):
                    term = arrived_ref[half * 8 + near * 4 + line, array].astype(F32)
                    total = term if total is None else total + term
            for end in range(2):
                for far in range(2):
                    rows = total[end * 4 : end * 4 + 4, far * width : (far + 1) * width]
                    out_ref[end * 4 + far * 2 + near, array] = rows.astype(BF16)


def plane_sums(arrived):
    width = arrived.shape[3] // 2
    return pl.pallas_call(
        sum_kernel,
        out_shape=jax.ShapeDtypeStruct((8, 2, 4, width), BF16),
        in_specs=[pl.BlockSpec(memory_space=pltpu.VMEM)],
        out_specs=pl.BlockSpec(memory_space=pltpu.VMEM),
        compiler_params=pltpu.CompilerParams(vmem_limit_bytes=VMEM_BYTES),
        cost_estimate=pl.CostEstimate(flops=800_000, bytes_accessed=1_800_000, transcendentals=0),
        name="plane_sums",
    )(arrived)


def local(tokens, up_proj, down_proj, out_grad):
    width = tokens.shape[1]
    units = down_proj.shape[0]
    member = lax.axis_index(GROUP).reshape(1).astype(jnp.int32)

    pieces = cut(member, up_proj.T, down_proj)
    beside = [other_core(pieces[0])]

    sideways = partner(pieces[2], GROUP, 4, 2)
    both = after(jnp.concatenate([tokens, out_grad], axis=0), beside[0])
    column = spread(both, COLUMN, 8)
    block = lax.axis_index(("z2", "z1")).reshape(1).astype(jnp.int32)
    sent, mine = lay_out(block, column)
    plane = exchange(sent, PLANE)

    own = [pieces[0], partner(after(pieces[1], column), GROUP, 4, 1), sideways]
    own.append(partner(after(pieces[3], column), GROUP, 4, 3))
    rows = blocks_of(mine, ("xh", "xp"), 4)
    waits = own[1:] + rows
    for piece in own[1:]:
        beside.append(other_core(after(piece, *waits)))
        waits = beside[1:2]

    flat = in_order(rows, ("xh", "xp"), 1)
    parts = hidden_parts(after(member, flat), plane, own, beside)
    arrived = exchange(parts, GROUP)
    flats = blocks_of(after(flat, parts), "y", 4)

    partials, pair = output_parts(after(member, *flats), arrived, own, beside, 16)
    arrived = exchange(partials, PLANE)
    summed = plane_sums(arrived)
    ends = jnp.sum(exchange(summed, COLUMN).astype(F32), axis=0).astype(BF16)

    flat = in_order(flats, "y", 2, partials).reshape(2, 128, width)
    flat = jnp.concatenate([flat, other_core(flat)], axis=1)
    lines = in_order(blocks_of(pair, ("z2", "z1"), 4), ("z2", "z1"), 2, arrived)
    lines = lines.reshape(2, 2, 8 * units, 128)
    units_all = jnp.concatenate([lines[0], other_core(lines[1])], axis=2)
    down_grad = dot(units_all[0], flat[1], 1, 0).astype(BF16)
    up_grad = dot(flat[0], units_all[1], 0, 1).astype(BF16)
    return (ends[0], ends[1], up_grad, down_grad)


def solution(mesh):
    fine = Mesh(
        mesh.devices.reshape(2, 2, 2, 4, 2, 2, 2, 2),
        ("xh", "xp", "zh", "y", "c", "z2", "z1", "zp"),
    )
    owners = ("xh", "xp", "zh", "y", "c")
    features = ("z2", "z1", "zp")
    return jax.shard_map(
        local,
        mesh=fine,
        in_specs=(
            P(owners, features),
            P(None, owners + features),
            P(owners + features, None),
            P(owners, features),
        ),
        out_specs=(
            P(owners, features),
            P(owners, features),
            P(features, owners),
            P(owners, features),
        ),
        check_vma=False,
    )
```

```python
import jax
import jax.numpy as jnp
from jax import lax
from jax.experimental import pallas as pl
from jax.experimental.pallas import tpu as pltpu
from jax.sharding import Mesh, PartitionSpec as P

BF16 = jnp.bfloat16
F32 = jnp.float32
VMEM_BYTES = 20 * 1024 * 1024

PLANE = ("xh", "xp", "y")
COLUMN = ("zh", "z2", "z1")
GROUP = ("xp", "zp")
STEPS = (0, 2, 3, 1)


def activate(values):
    return jax.nn.gelu(values, approximate=True)


def gelu_slope(pre_act, cotangent):
    unused, pullback = jax.vjp(activate, pre_act)
    return pullback(cotangent)[0]


def exchange(value, axes):
    return lax.all_to_all(value, axes, split_axis=0, concat_axis=0, tiled=True)


def spread(value, axes, count):
    return exchange(jnp.broadcast_to(value[None], (count,) + value.shape), axes)


def partner(value, axes, count, step):
    return lax.ppermute(value, axes, [(at, at ^ step) for at in range(count)])


def other_core(value):
    return partner(value, "c", 2, 1)


def gather_ring(value, axes, count, dim, *others):
    here = lax.axis_index(axes)
    shape = list(value.shape)
    shape[dim] = count
    start = [0] * len(shape)
    whole = jnp.zeros(shape, value.dtype)
    blocks = [value] + [partner(value, axes, count, step) for step in range(1, count)]
    for step, block in enumerate(lax.optimization_barrier(blocks + list(others))[:count]):
        start[dim] = here ^ step
        whole = lax.dynamic_update_slice(whole, block, tuple(start))
    return whole


def after(value, *others):
    return lax.optimization_barrier((value,) + others)[0]


def dot(left, right, left_dim, right_dim):
    return lax.dot_general(
        left, right, (((left_dim,), (right_dim,)), ((), ())), preferred_element_type=F32
    )


def cut_kernel(member_ref, up_ref, down_ref, *pieces):
    width = pieces[0].shape[2] // 2
    for at, step in enumerate(STEPS):
        for kind, source in enumerate((up_ref, down_ref)):
            for far in range(2):
                column = pl.multiple_of((far * 4 + (member_ref[0] ^ step)) * width, width)
                pieces[at][kind, :, far * width : (far + 1) * width] = source[:, pl.ds(column, width)]


def cut(member, up_rows, down_rows):
    units, features = up_rows.shape
    piece = jax.ShapeDtypeStruct((2, units, features // 4), BF16)
    return pl.pallas_call(
        cut_kernel,
        out_shape=[piece] * 4,
        in_specs=[pl.BlockSpec(memory_space=pltpu.SMEM)] + [pl.BlockSpec(memory_space=pltpu.VMEM)] * 2,
        out_specs=[pl.BlockSpec(memory_space=pltpu.VMEM)] * 4,
        compiler_params=pltpu.CompilerParams(vmem_limit_bytes=VMEM_BYTES),
        cost_estimate=pl.CostEstimate(flops=0, bytes_accessed=8 * units * features, transcendentals=0),
        name="cut_weights",
    )(member, up_rows, down_rows)


def lay_out_kernel(block_ref, column_ref, sent_ref):
    def rows_of(at, array):
        ends = [column_ref[end * 4 + at, array * 4 : array * 4 + 4].astype(F32) for end in range(2)]
        return jnp.concatenate(ends, axis=0).astype(BF16)

    for array in range(2):
        own = rows_of(block_ref[0], array)
        for near in range(2):
            blocks = [rows_of(far * 2 + near, array) for far in range(2)] + [own]
            for half in range(2):
                for line in range(4):
                    for far in range(3):
                        sent_ref[half * 8 + near * 4 + line, far, array] = blocks[far]


def lay_out(block, column):
    unused, rows, width = column.shape
    return pl.pallas_call(
        lay_out_kernel,
        out_shape=jax.ShapeDtypeStruct((16, 3, 2, rows, width), BF16),
        in_specs=[pl.BlockSpec(memory_space=pltpu.SMEM), pl.BlockSpec(memory_space=pltpu.VMEM)],
        out_specs=pl.BlockSpec(memory_space=pltpu.VMEM),
        compiler_params=pltpu.CompilerParams(vmem_limit_bytes=VMEM_BYTES),
        cost_estimate=pl.CostEstimate(flops=0, bytes_accessed=2_800_000, transcendentals=0),
        name="lay_out_rows",
    )(block, column)


def hidden_kernel(member_ref, rows_ref, *refs):
    own, beside, out_ref, mine_ref = refs[:4], refs[4:8], refs[8], refs[9]
    units = own[0].shape[1]
    width = rows_ref.shape[4]
    for kind in range(2):
        rows = [rows_ref[:, far, kind].reshape(-1, width) for far in range(3)]
        mine_ref[kind] = rows[2]
        for core, pieces in enumerate((own, beside)):
            total = None
            for far in range(2):
                weight = jnp.concatenate(
                    [piece[kind, :, far * width : (far + 1) * width] for piece in pieces], axis=0
                )
                term = dot(weight, rows[far], 1, 1)
                total = term if total is None else total + term
            sends = [(kind, total.astype(BF16))]
            if kind == 0:
                sends.append((2, (total - sends[0][1].astype(F32)).astype(BF16)))
            for row, value in sends:
                for place, step in enumerate(STEPS):
                    for at in range(4):
                        out_ref[at, member_ref[0] ^ step, row, core] = value[place * units : (place + 1) * units]


def hidden_parts(member, rows, own, beside):
    units = own[0].shape[1]
    tokens = rows.shape[0] * rows.shape[3]
    return pl.pallas_call(
        hidden_kernel,
        out_shape=[
            jax.ShapeDtypeStruct((4, 4, 3, 2, units, tokens), BF16),
            jax.ShapeDtypeStruct((2, tokens, rows.shape[4]), BF16),
        ],
        in_specs=[pl.BlockSpec(memory_space=pltpu.SMEM)] + [pl.BlockSpec(memory_space=pltpu.VMEM)] * 9,
        out_specs=[pl.BlockSpec(memory_space=pltpu.VMEM)] * 2,
        compiler_params=pltpu.CompilerParams(vmem_limit_bytes=VMEM_BYTES),
        cost_estimate=pl.CostEstimate(flops=604_000_000, bytes_accessed=6_700_000, transcendentals=0),
        name="hidden_parts",
    )(member, rows, *own, *beside)


def output_kernel(member_ref, parts_ref, *refs):
    own, beside, out_ref, pair_ref = refs[:4], refs[4:8], refs[8], refs[9]
    features = own[0].shape[2]
    count, unused, rows, unused = out_ref.shape
    step_of = features // 4
    units = [[], []]
    for core in range(2):
        for step in STEPS:
            slot = member_ref[0] ^ step
            value, act_grad, rest = (
                sum(parts_ref[source, slot, row, core].astype(F32) for source in range(4)) for row in range(3)
            )
            pre_act = value + rest
            values = (activate(pre_act).astype(BF16), gelu_slope(pre_act, act_grad).astype(BF16))
            for kind in range(2):
                units[kind].append(values[kind])
                if step < 2:
                    pair_ref[core, kind, 0, slot % 2] = values[kind]
    for result in range(2):
        left = jnp.concatenate(units[result], axis=0)
        for at in range(4):
            columns = slice(at * step_of, (at + 1) * step_of)
            weight = jnp.concatenate(
                [piece[1 - result, :, columns] for piece in (*own, *beside)], axis=0
            )
            total = dot(left, weight, 0, 0)
            out_ref[:, result, :, columns] = total.astype(BF16).reshape(count, rows, step_of)


def output_parts(member, parts, own, beside, count):
    features = own[0].shape[2]
    units, tokens = parts.shape[4:]
    return pl.pallas_call(
        output_kernel,
        out_shape=[
            jax.ShapeDtypeStruct((count, 2, tokens // count, features), BF16),
            jax.ShapeDtypeStruct((2, 2, 1, 2, units, tokens), BF16),
        ],
        in_specs=[pl.BlockSpec(memory_space=pltpu.SMEM)] + [pl.BlockSpec(memory_space=pltpu.VMEM)] * 9,
        out_specs=[pl.BlockSpec(memory_space=pltpu.VMEM)] * 2,
        compiler_params=pltpu.CompilerParams(vmem_limit_bytes=VMEM_BYTES),
        cost_estimate=pl.CostEstimate(flops=604_000_000, bytes_accessed=6_700_000, transcendentals=49_152),
        name="output_parts",
    )(member, parts, *own, *beside)


def sum_kernel(arrived_ref, out_ref):
    width = out_ref.shape[3]
    for near in range(2):
        for array in range(2):
            total = None
            for half in range(2):
                for line in range(4):
                    term = arrived_ref[half * 8 + near * 4 + line, array].astype(F32)
                    total = term if total is None else total + term
            for end in range(2):
                for far in range(2):
                    rows = total[end * 4 : end * 4 + 4, far * width : (far + 1) * width]
                    out_ref[end * 4 + far * 2 + near, array] = rows.astype(BF16)


def plane_sums(arrived):
    width = arrived.shape[3] // 2
    return pl.pallas_call(
        sum_kernel,
        out_shape=jax.ShapeDtypeStruct((8, 2, 4, width), BF16),
        in_specs=[pl.BlockSpec(memory_space=pltpu.VMEM)],
        out_specs=pl.BlockSpec(memory_space=pltpu.VMEM),
        compiler_params=pltpu.CompilerParams(vmem_limit_bytes=VMEM_BYTES),
        cost_estimate=pl.CostEstimate(flops=800_000, bytes_accessed=1_800_000, transcendentals=0),
        name="plane_sums",
    )(arrived)


def local(tokens, up_proj, down_proj, out_grad):
    width = tokens.shape[1]
    units = down_proj.shape[0]
    member = lax.axis_index(GROUP).reshape(1).astype(jnp.int32)

    pieces = cut(member, up_proj.T, down_proj)
    own = [pieces[0]] + [partner(pieces[at], GROUP, 4, STEPS[at]) for at in range(1, 4)]
    beside = [other_core(pieces[0])]
    waits = own[1:]
    for piece in own[1:]:
        beside.append(other_core(after(piece, *waits)))
        waits = beside[-1:]

    both = jnp.concatenate([tokens, out_grad], axis=0)
    column = spread(both, COLUMN, 8)
    block = lax.axis_index(("z2", "z1")).reshape(1).astype(jnp.int32)
    sent = lay_out(block, column)
    plane = exchange(sent, PLANE)

    parts, mine = hidden_parts(member, plane, own, beside)
    arrived = exchange(parts, GROUP)

    partials, pair = output_parts(member, arrived, own, beside, 16)
    arrived = exchange(partials, PLANE)
    summed = plane_sums(arrived)
    ends = jnp.sum(exchange(summed, COLUMN).astype(F32), axis=0).astype(BF16)

    flat = jnp.concatenate([mine, other_core(mine)], axis=1)
    lines = gather_ring(pair, ("z2", "z1"), 4, 2, arrived)
    lines = lines.reshape(2, 2, 8 * units, 128)
    units_all = jnp.concatenate([lines[0], other_core(lines[1])], axis=2)
    down_grad = dot(units_all[0], flat[1], 1, 0).astype(BF16)
    up_grad = dot(flat[0], units_all[1], 0, 1).astype(BF16)
    return (ends[0], ends[1], up_grad, down_grad)


def solution(mesh):
    fine = Mesh(
        mesh.devices.reshape(2, 2, 2, 4, 2, 2, 2, 2),
        ("xh", "xp", "zh", "y", "c", "z2", "z1", "zp"),
    )
    owners = ("xh", "xp", "zh", "y", "c")
    features = ("z2", "z1", "zp")
    return jax.shard_map(
        local,
        mesh=fine,
        in_specs=(
            P(owners, features),
            P(None, owners + features),
            P(owners + features, None),
            P(owners, features),
        ),
        out_specs=(
            P(owners, features),
            P(owners, features),
            P(features, owners),
            P(owners, features),
        ),
        check_vma=False,
    )
```

```python
import jax
import jax.numpy as jnp
from jax import lax
from jax.experimental import pallas as pl
from jax.experimental.pallas import tpu as pltpu
from jax.sharding import Mesh, PartitionSpec as P

BF16 = jnp.bfloat16
F32 = jnp.float32
VMEM_BYTES = 20 * 1024 * 1024

PLANE = ("xh", "xp", "y")
COLUMN = ("zh", "z2", "z1")
GROUP = ("xp", "zp")
STEPS = (0, 2, 3, 1)


def activate(values):
    return jax.nn.gelu(values, approximate=True)


def gelu_slope(pre_act, cotangent):
    unused, pullback = jax.vjp(activate, pre_act)
    return pullback(cotangent)[0]


def exchange(value, axes):
    return lax.all_to_all(value, axes, split_axis=0, concat_axis=0, tiled=True)


def spread(value, axes, count):
    return exchange(jnp.broadcast_to(value[None], (count,) + value.shape), axes)


def partner(value, axes, count, step):
    return lax.ppermute(value, axes, [(at, at ^ step) for at in range(count)])


def other_core(value):
    return partner(value, "c", 2, 1)


def gather_ring(value, axes, count, dim, *others):
    here = lax.axis_index(axes)
    shape = list(value.shape)
    shape[dim] = count
    start = [0] * len(shape)
    whole = jnp.zeros(shape, value.dtype)
    blocks = [value] + [partner(value, axes, count, step) for step in range(1, count)]
    for step, block in enumerate(lax.optimization_barrier(blocks + list(others))[:count]):
        start[dim] = here ^ step
        whole = lax.dynamic_update_slice(whole, block, tuple(start))
    return whole


def after(value, *others):
    return lax.optimization_barrier((value,) + others)[0]


def dot(left, right, left_dim, right_dim):
    return lax.dot_general(
        left, right, (((left_dim,), (right_dim,)), ((), ())), preferred_element_type=F32
    )


def cut_kernel(member_ref, up_ref, down_ref, *pieces):
    width = pieces[0].shape[2] // 2
    for at, step in enumerate(STEPS):
        for kind, source in enumerate((up_ref, down_ref)):
            for far in range(2):
                column = pl.multiple_of((far * 4 + (member_ref[0] ^ step)) * width, width)
                pieces[at][kind, :, far * width : (far + 1) * width] = source[:, pl.ds(column, width)]


def cut(member, up_rows, down_rows):
    units, features = up_rows.shape
    piece = jax.ShapeDtypeStruct((2, units, features // 4), BF16)
    return pl.pallas_call(
        cut_kernel,
        out_shape=[piece] * 4,
        in_specs=[pl.BlockSpec(memory_space=pltpu.SMEM)] + [pl.BlockSpec(memory_space=pltpu.VMEM)] * 2,
        out_specs=[pl.BlockSpec(memory_space=pltpu.VMEM)] * 4,
        compiler_params=pltpu.CompilerParams(vmem_limit_bytes=VMEM_BYTES),
        cost_estimate=pl.CostEstimate(flops=0, bytes_accessed=8 * units * features, transcendentals=0),
        name="cut_weights",
    )(member, up_rows, down_rows)


def lay_out_kernel(block_ref, column_ref, sent_ref):
    def rows_of(at, array):
        ends = [column_ref[end * 4 + at, array * 4 : array * 4 + 4].astype(F32) for end in range(2)]
        return jnp.concatenate(ends, axis=0).astype(BF16)

    for array in range(2):
        own = rows_of(block_ref[0], array)
        for near in range(2):
            blocks = [rows_of(far * 2 + near, array) for far in range(2)] + [own]
            for half in range(2):
                for line in range(4):
                    for far in range(3):
                        sent_ref[half * 8 + near * 4 + line, far, array] = blocks[far]


def lay_out(block, column):
    unused, rows, width = column.shape
    return pl.pallas_call(
        lay_out_kernel,
        out_shape=jax.ShapeDtypeStruct((16, 3, 2, rows, width), BF16),
        in_specs=[pl.BlockSpec(memory_space=pltpu.SMEM), pl.BlockSpec(memory_space=pltpu.VMEM)],
        out_specs=pl.BlockSpec(memory_space=pltpu.VMEM),
        compiler_params=pltpu.CompilerParams(vmem_limit_bytes=VMEM_BYTES),
        cost_estimate=pl.CostEstimate(flops=0, bytes_accessed=2_800_000, transcendentals=0),
        name="lay_out_rows",
    )(block, column)


def hidden_kernel(member_ref, source_ref, *refs):
    pieces, (out_ref, mine_ref, rows_ref, held_ref, sems) = refs[:8], refs[8:]
    units = pieces[0].shape[1]
    width = rows_ref.shape[4]
    copies = [pltpu.make_async_copy(source_ref, rows_ref, sems.at[8])]
    copies += [pltpu.make_async_copy(pieces[at], held_ref.at[at], sems.at[at]) for at in range(8)]
    for copy in copies:
        copy.start()
    for copy in copies:
        copy.wait()
    own, beside = ([held_ref.at[core * 4 + at] for at in range(4)] for core in range(2))
    for kind in range(2):
        rows = [rows_ref[:, far, kind].reshape(-1, width) for far in range(3)]
        mine_ref[kind] = rows[2]
        for core, pieces in enumerate((own, beside)):
            total = None
            for far in range(2):
                weight = jnp.concatenate(
                    [piece[kind, :, far * width : (far + 1) * width] for piece in pieces], axis=0
                )
                term = dot(weight, rows[far], 1, 1)
                total = term if total is None else total + term
            sends = [(kind, total.astype(BF16))]
            if kind == 0:
                sends.append((2, (total - sends[0][1].astype(F32)).astype(BF16)))
            for row, value in sends:
                for place, step in enumerate(STEPS):
                    for at in range(4):
                        out_ref[at, member_ref[0] ^ step, row, core] = value[place * units : (place + 1) * units]


def hidden_parts(member, rows, own, beside):
    units = own[0].shape[1]
    tokens = rows.shape[0] * rows.shape[3]
    return pl.pallas_call(
        hidden_kernel,
        out_shape=[
            jax.ShapeDtypeStruct((4, 4, 3, 2, units, tokens), BF16),
            jax.ShapeDtypeStruct((2, tokens, rows.shape[4]), BF16),
        ],
        in_specs=[pl.BlockSpec(memory_space=pltpu.SMEM)] + [pl.BlockSpec(memory_space=pltpu.HBM)] * 9,
        out_specs=[pl.BlockSpec(memory_space=pltpu.VMEM)] * 2,
        scratch_shapes=[
            pltpu.VMEM(rows.shape, BF16),
            pltpu.VMEM((8,) + own[0].shape, BF16),
            pltpu.SemaphoreType.DMA((9,)),
        ],
        compiler_params=pltpu.CompilerParams(vmem_limit_bytes=3 * VMEM_BYTES),
        cost_estimate=pl.CostEstimate(flops=604_000_000, bytes_accessed=6_700_000, transcendentals=0),
        name="hidden_parts",
    )(member, rows, *own, *beside)


def output_kernel(member_ref, parts_ref, *refs):
    own, beside, out_ref, pair_ref = refs[:4], refs[4:8], refs[8], refs[9]
    features = own[0].shape[2]
    count, unused, rows, unused = out_ref.shape
    step_of = features // 4
    units = [[], []]
    for core in range(2):
        for step in STEPS:
            slot = member_ref[0] ^ step
            value, act_grad, rest = (
                sum(parts_ref[source, slot, row, core].astype(F32) for source in range(4)) for row in range(3)
            )
            pre_act = value + rest
            values = (activate(pre_act).astype(BF16), gelu_slope(pre_act, act_grad).astype(BF16))
            for kind in range(2):
                units[kind].append(values[kind])
                if step < 2:
                    pair_ref[core, kind, 0, slot % 2] = values[kind]
    for result in range(2):
        left = jnp.concatenate(units[result], axis=0)
        for at in range(4):
            columns = slice(at * step_of, (at + 1) * step_of)
            weight = jnp.concatenate(
                [piece[1 - result, :, columns] for piece in (*own, *beside)], axis=0
            )
            total = dot(left, weight, 0, 0)
            out_ref[:, result, :, columns] = total.astype(BF16).reshape(count, rows, step_of)


def output_parts(member, parts, own, beside, count):
    features = own[0].shape[2]
    units, tokens = parts.shape[4:]
    return pl.pallas_call(
        output_kernel,
        out_shape=[
            jax.ShapeDtypeStruct((count, 2, tokens // count, features), BF16),
            jax.ShapeDtypeStruct((2, 2, 1, 2, units, tokens), BF16),
        ],
        in_specs=[pl.BlockSpec(memory_space=pltpu.SMEM)] + [pl.BlockSpec(memory_space=pltpu.VMEM)] * 9,
        out_specs=[pl.BlockSpec(memory_space=pltpu.VMEM)] * 2,
        compiler_params=pltpu.CompilerParams(vmem_limit_bytes=VMEM_BYTES),
        cost_estimate=pl.CostEstimate(flops=604_000_000, bytes_accessed=6_700_000, transcendentals=49_152),
        name="output_parts",
    )(member, parts, *own, *beside)


def sum_kernel(arrived_ref, out_ref):
    width = out_ref.shape[3]
    for near in range(2):
        for array in range(2):
            total = None
            for half in range(2):
                for line in range(4):
                    term = arrived_ref[half * 8 + near * 4 + line, array].astype(F32)
                    total = term if total is None else total + term
            for end in range(2):
                for far in range(2):
                    rows = total[end * 4 : end * 4 + 4, far * width : (far + 1) * width]
                    out_ref[end * 4 + far * 2 + near, array] = rows.astype(BF16)


def plane_sums(arrived):
    width = arrived.shape[3] // 2
    return pl.pallas_call(
        sum_kernel,
        out_shape=jax.ShapeDtypeStruct((8, 2, 4, width), BF16),
        in_specs=[pl.BlockSpec(memory_space=pltpu.VMEM)],
        out_specs=pl.BlockSpec(memory_space=pltpu.VMEM),
        compiler_params=pltpu.CompilerParams(vmem_limit_bytes=VMEM_BYTES),
        cost_estimate=pl.CostEstimate(flops=800_000, bytes_accessed=1_800_000, transcendentals=0),
        name="plane_sums",
    )(arrived)


def local(tokens, up_proj, down_proj, out_grad):
    width = tokens.shape[1]
    units = down_proj.shape[0]
    member = lax.axis_index(GROUP).reshape(1).astype(jnp.int32)

    pieces = cut(member, up_proj.T, down_proj)
    own = [pieces[0]] + [partner(pieces[at], GROUP, 4, STEPS[at]) for at in range(1, 4)]
    beside = [other_core(pieces[0])]
    waits = own[1:]
    for piece in own[1:]:
        beside.append(other_core(after(piece, *waits)))
        waits = beside[-1:]

    both = jnp.concatenate([tokens, out_grad], axis=0)
    column = spread(both, COLUMN, 8)
    block = lax.axis_index(("z2", "z1")).reshape(1).astype(jnp.int32)
    sent = lay_out(block, column)
    plane = exchange(sent, PLANE)

    parts, mine = hidden_parts(member, plane, own, beside)
    arrived = exchange(parts, GROUP)

    partials, pair = output_parts(member, arrived, own, beside, 16)
    arrived = exchange(partials, PLANE)
    summed = plane_sums(arrived)
    ends = jnp.sum(exchange(summed, COLUMN).astype(F32), axis=0).astype(BF16)

    flat = jnp.concatenate([mine, other_core(mine)], axis=1)
    lines = gather_ring(pair, ("z2", "z1"), 4, 2, arrived)
    lines = lines.reshape(2, 2, 8 * units, 128)
    units_all = jnp.concatenate([lines[0], other_core(lines[1])], axis=2)
    down_grad = dot(units_all[0], flat[1], 1, 0).astype(BF16)
    up_grad = dot(flat[0], units_all[1], 0, 1).astype(BF16)
    return (ends[0], ends[1], up_grad, down_grad)


def solution(mesh):
    fine = Mesh(
        mesh.devices.reshape(2, 2, 2, 4, 2, 2, 2, 2),
        ("xh", "xp", "zh", "y", "c", "z2", "z1", "zp"),
    )
    owners = ("xh", "xp", "zh", "y", "c")
    features = ("z2", "z1", "zp")
    return jax.shard_map(
        local,
        mesh=fine,
        in_specs=(
            P(owners, features),
            P(None, owners + features),
            P(owners + features, None),
            P(owners, features),
        ),
        out_specs=(
            P(owners, features),
            P(owners, features),
            P(features, owners),
            P(owners, features),
        ),
        check_vma=False,
    )
```

```python
import jax
import jax.numpy as jnp
from jax import lax
from jax.experimental import pallas as pl
from jax.experimental.pallas import tpu as pltpu
from jax.sharding import Mesh, PartitionSpec as P

BF16 = jnp.bfloat16
F32 = jnp.float32
VMEM_BYTES = 20 * 1024 * 1024

PLANE = ("xh", "xp", "y")
COLUMN = ("zh", "z2", "z1")
GROUP = ("xp", "zp")
STEPS = (0, 2, 3, 1)


def activate(values):
    return jax.nn.gelu(values, approximate=True)


def gelu_slope(pre_act, cotangent):
    unused, pullback = jax.vjp(activate, pre_act)
    return pullback(cotangent)[0]


def exchange(value, axes):
    return lax.all_to_all(value, axes, split_axis=0, concat_axis=0, tiled=True)


def spread(value, axes, count):
    return exchange(jnp.broadcast_to(value[None], (count,) + value.shape), axes)


def partner(value, axes, count, step):
    return lax.ppermute(value, axes, [(at, at ^ step) for at in range(count)])


def other_core(value):
    return partner(value, "c", 2, 1)


def gather_ring(value, axes, count, dim, *others):
    here = lax.axis_index(axes)
    shape = list(value.shape)
    shape[dim] = count
    start = [0] * len(shape)
    whole = jnp.zeros(shape, value.dtype)
    blocks = [value] + [partner(value, axes, count, step) for step in range(1, count)]
    for step, block in enumerate(lax.optimization_barrier(blocks + list(others))[:count]):
        start[dim] = here ^ step
        whole = lax.dynamic_update_slice(whole, block, tuple(start))
    return whole


def after(value, *others):
    return lax.optimization_barrier((value,) + others)[0]


def dot(left, right, left_dim, right_dim):
    return lax.dot_general(
        left, right, (((left_dim,), (right_dim,)), ((), ())), preferred_element_type=F32
    )


def cut_kernel(member_ref, up_ref, down_ref, *pieces):
    width = pieces[0].shape[2] // 2
    for at, step in enumerate(STEPS):
        for kind, source in enumerate((up_ref, down_ref)):
            for far in range(2):
                column = pl.multiple_of((far * 4 + (member_ref[0] ^ step)) * width, width)
                pieces[at][kind, :, far * width : (far + 1) * width] = source[:, pl.ds(column, width)]


def cut(member, up_rows, down_rows):
    units, features = up_rows.shape
    piece = jax.ShapeDtypeStruct((2, units, features // 4), BF16)
    return pl.pallas_call(
        cut_kernel,
        out_shape=[piece] * 4,
        in_specs=[pl.BlockSpec(memory_space=pltpu.SMEM)] + [pl.BlockSpec(memory_space=pltpu.VMEM)] * 2,
        out_specs=[pl.BlockSpec(memory_space=pltpu.VMEM)] * 4,
        compiler_params=pltpu.CompilerParams(vmem_limit_bytes=VMEM_BYTES),
        cost_estimate=pl.CostEstimate(flops=0, bytes_accessed=8 * units * features, transcendentals=0),
        name="cut_weights",
    )(member, up_rows, down_rows)


def lay_out_kernel(block_ref, column_ref, sent_ref):
    def rows_of(at, array):
        ends = [column_ref[end * 4 + at, array * 4 : array * 4 + 4].astype(F32) for end in range(2)]
        return jnp.concatenate(ends, axis=0).astype(BF16)

    for array in range(2):
        own = rows_of(block_ref[0], array)
        for near in range(2):
            blocks = [rows_of(far * 2 + near, array) for far in range(2)] + [own]
            for half in range(2):
                for line in range(4):
                    for far in range(3):
                        sent_ref[half * 8 + near * 4 + line, far, array] = blocks[far]


def lay_out(block, column):
    unused, rows, width = column.shape
    return pl.pallas_call(
        lay_out_kernel,
        out_shape=jax.ShapeDtypeStruct((16, 3, 2, rows, width), BF16),
        in_specs=[pl.BlockSpec(memory_space=pltpu.SMEM), pl.BlockSpec(memory_space=pltpu.VMEM)],
        out_specs=pl.BlockSpec(memory_space=pltpu.VMEM),
        compiler_params=pltpu.CompilerParams(vmem_limit_bytes=VMEM_BYTES),
        cost_estimate=pl.CostEstimate(flops=0, bytes_accessed=2_800_000, transcendentals=0),
        name="lay_out_rows",
    )(block, column)


def hidden_kernel(member_ref, source_ref, *refs):
    pieces, (out_ref, mine_ref, rows_ref, held_ref, sems) = refs[:8], refs[8:]
    units = pieces[0].shape[1]
    width = rows_ref.shape[4]
    copies = [pltpu.make_async_copy(source_ref, rows_ref, sems.at[8])]
    copies += [pltpu.make_async_copy(pieces[at], held_ref.at[at], sems.at[at]) for at in range(8)]
    for copy in copies:
        copy.start()
    copies[0].wait()
    for core in range(2):
        held = [held_ref.at[core * 4 + at] for at in range(4)]
        for copy in copies[1 + core * 4 : 5 + core * 4]:
            copy.wait()
        for kind in range(2):
            rows = [rows_ref[:, far, kind].reshape(-1, width) for far in range(2)]
            if core == 0:
                mine_ref[kind] = rows_ref[:, 2, kind].reshape(-1, width)
            total = None
            for far in range(2):
                weight = jnp.concatenate(
                    [piece[kind, :, far * width : (far + 1) * width] for piece in held], axis=0
                )
                term = dot(weight, rows[far], 1, 1)
                total = term if total is None else total + term
            sends = [(kind, total.astype(BF16))]
            if kind == 0:
                sends.append((2, (total - sends[0][1].astype(F32)).astype(BF16)))
            for row, value in sends:
                for place, step in enumerate(STEPS):
                    for at in range(4):
                        out_ref[at, member_ref[0] ^ step, row, core] = value[place * units : (place + 1) * units]


def hidden_parts(member, rows, own, beside):
    units = own[0].shape[1]
    tokens = rows.shape[0] * rows.shape[3]
    return pl.pallas_call(
        hidden_kernel,
        out_shape=[
            jax.ShapeDtypeStruct((4, 4, 3, 2, units, tokens), BF16),
            jax.ShapeDtypeStruct((2, tokens, rows.shape[4]), BF16),
        ],
        in_specs=[pl.BlockSpec(memory_space=pltpu.SMEM)] + [pl.BlockSpec(memory_space=pltpu.HBM)] * 9,
        out_specs=[pl.BlockSpec(memory_space=pltpu.VMEM)] * 2,
        scratch_shapes=[
            pltpu.VMEM(rows.shape, BF16),
            pltpu.VMEM((8,) + own[0].shape, BF16),
            pltpu.SemaphoreType.DMA((9,)),
        ],
        compiler_params=pltpu.CompilerParams(vmem_limit_bytes=3 * VMEM_BYTES),
        cost_estimate=pl.CostEstimate(flops=604_000_000, bytes_accessed=6_700_000, transcendentals=0),
        name="hidden_parts",
    )(member, rows, *own, *beside)


def output_kernel(member_ref, parts_ref, *refs):
    pieces, (out_ref, pair_ref, held_ref, sems) = refs[:8], refs[8:]
    copies = [pltpu.make_async_copy(pieces[at], held_ref.at[at], sems.at[at]) for at in range(8)]
    for copy in copies:
        copy.start()
    features = pieces[0].shape[2]
    count, unused, rows, unused = out_ref.shape
    step_of = features // 4
    units = [[], []]
    for core in range(2):
        for step in STEPS:
            slot = member_ref[0] ^ step
            value, act_grad, rest = (
                sum(parts_ref[source, slot, row, core].astype(F32) for source in range(4)) for row in range(3)
            )
            pre_act = value + rest
            values = (activate(pre_act).astype(BF16), gelu_slope(pre_act, act_grad).astype(BF16))
            for kind in range(2):
                units[kind].append(values[kind])
                if step < 2:
                    pair_ref[core, kind, 0, slot % 2] = values[kind]
    for copy in copies:
        copy.wait()
    for result in range(2):
        left = jnp.concatenate(units[result], axis=0)
        for cut_at in range(4):
            columns = slice(cut_at * step_of, (cut_at + 1) * step_of)
            weight = jnp.concatenate(
                [held_ref[at, 1 - result, :, columns] for at in range(8)], axis=0
            )
            total = dot(left, weight, 0, 0)
            out_ref[:, result, :, columns] = total.astype(BF16).reshape(count, rows, step_of)


def output_parts(member, parts, own, beside, count):
    features = own[0].shape[2]
    units, tokens = parts.shape[4:]
    return pl.pallas_call(
        output_kernel,
        out_shape=[
            jax.ShapeDtypeStruct((count, 2, tokens // count, features), BF16),
            jax.ShapeDtypeStruct((2, 2, 1, 2, units, tokens), BF16),
        ],
        in_specs=[pl.BlockSpec(memory_space=pltpu.SMEM), pl.BlockSpec(memory_space=pltpu.VMEM)]
        + [pl.BlockSpec(memory_space=pltpu.HBM)] * 8,
        out_specs=[pl.BlockSpec(memory_space=pltpu.VMEM)] * 2,
        scratch_shapes=[pltpu.VMEM((8,) + own[0].shape, BF16), pltpu.SemaphoreType.DMA((8,))],
        compiler_params=pltpu.CompilerParams(vmem_limit_bytes=3 * VMEM_BYTES),
        cost_estimate=pl.CostEstimate(flops=604_000_000, bytes_accessed=6_700_000, transcendentals=49_152),
        name="output_parts",
    )(member, parts, *own, *beside)


def sum_kernel(arrived_ref, out_ref):
    width = out_ref.shape[3]
    for near in range(2):
        for array in range(2):
            total = None
            for half in range(2):
                for line in range(4):
                    term = arrived_ref[half * 8 + near * 4 + line, array].astype(F32)
                    total = term if total is None else total + term
            for end in range(2):
                for far in range(2):
                    rows = total[end * 4 : end * 4 + 4, far * width : (far + 1) * width]
                    out_ref[end * 4 + far * 2 + near, array] = rows.astype(BF16)


def plane_sums(arrived):
    width = arrived.shape[3] // 2
    return pl.pallas_call(
        sum_kernel,
        out_shape=jax.ShapeDtypeStruct((8, 2, 4, width), BF16),
        in_specs=[pl.BlockSpec(memory_space=pltpu.VMEM)],
        out_specs=pl.BlockSpec(memory_space=pltpu.VMEM),
        compiler_params=pltpu.CompilerParams(vmem_limit_bytes=VMEM_BYTES),
        cost_estimate=pl.CostEstimate(flops=800_000, bytes_accessed=1_800_000, transcendentals=0),
        name="plane_sums",
    )(arrived)


def local(tokens, up_proj, down_proj, out_grad):
    width = tokens.shape[1]
    units = down_proj.shape[0]
    member = lax.axis_index(GROUP).reshape(1).astype(jnp.int32)

    pieces = cut(member, up_proj.T, down_proj)
    own = [pieces[0]] + [partner(pieces[at], GROUP, 4, STEPS[at]) for at in range(1, 4)]
    beside = [other_core(pieces[0])]
    waits = own[1:]
    for piece in own[1:]:
        beside.append(other_core(after(piece, *waits)))
        waits = beside[-1:]

    both = jnp.concatenate([tokens, out_grad], axis=0)
    column = spread(both, COLUMN, 8)
    block = lax.axis_index(("z2", "z1")).reshape(1).astype(jnp.int32)
    sent = lay_out(block, column)
    plane = exchange(sent, PLANE)

    parts, mine = hidden_parts(member, plane, own, beside)
    arrived = exchange(parts, GROUP)

    partials, pair = output_parts(member, arrived, own, beside, 16)
    arrived = exchange(partials, PLANE)
    summed = plane_sums(arrived)
    ends = jnp.sum(exchange(summed, COLUMN).astype(F32), axis=0).astype(BF16)

    flat = jnp.concatenate([mine, other_core(mine)], axis=1)
    lines = gather_ring(pair, ("z2", "z1"), 4, 2, arrived)
    lines = lines.reshape(2, 2, 8 * units, 128)
    units_all = jnp.concatenate([lines[0], other_core(lines[1])], axis=2)
    down_grad = dot(units_all[0], flat[1], 1, 0).astype(BF16)
    up_grad = dot(flat[0], units_all[1], 0, 1).astype(BF16)
    return (ends[0], ends[1], up_grad, down_grad)


def solution(mesh):
    fine = Mesh(
        mesh.devices.reshape(2, 2, 2, 4, 2, 2, 2, 2),
        ("xh", "xp", "zh", "y", "c", "z2", "z1", "zp"),
    )
    owners = ("xh", "xp", "zh", "y", "c")
    features = ("z2", "z1", "zp")
    return jax.shard_map(
        local,
        mesh=fine,
        in_specs=(
            P(owners, features),
            P(None, owners + features),
            P(owners + features, None),
            P(owners, features),
        ),
        out_specs=(
            P(owners, features),
            P(owners, features),
            P(features, owners),
            P(owners, features),
        ),
        check_vma=False,
    )
```

```python
import jax
import jax.numpy as jnp
from jax import lax
from jax.experimental import pallas as pl
from jax.experimental.pallas import tpu as pltpu
from jax.sharding import Mesh, PartitionSpec as P

BF16 = jnp.bfloat16
F32 = jnp.float32
VMEM_BYTES = 20 * 1024 * 1024

PLANE = ("xh", "xp", "y")
COLUMN = ("zh", "z2", "z1")
GROUP = ("xp", "zp")
STEPS = (0, 3, 2, 1)


def activate(values):
    return jax.nn.gelu(values, approximate=True)


def gelu_slope(pre_act, cotangent):
    unused, pullback = jax.vjp(activate, pre_act)
    return pullback(cotangent)[0]


def exchange(value, axes):
    return lax.all_to_all(value, axes, split_axis=0, concat_axis=0, tiled=True)


def spread(value, axes, count):
    return exchange(jnp.broadcast_to(value[None], (count,) + value.shape), axes)


def partner(value, axes, count, step):
    return lax.ppermute(value, axes, [(at, at ^ step) for at in range(count)])


def other_core(value):
    return partner(value, "c", 2, 1)


def gather_ring(value, axes, count, dim, *others):
    here = lax.axis_index(axes)
    shape = list(value.shape)
    shape[dim] = count
    start = [0] * len(shape)
    whole = jnp.zeros(shape, value.dtype)
    blocks = [value] + [partner(value, axes, count, step) for step in range(1, count)]
    for step, block in enumerate(lax.optimization_barrier(blocks + list(others))[:count]):
        start[dim] = here ^ step
        whole = lax.dynamic_update_slice(whole, block, tuple(start))
    return whole


def after(value, *others):
    return lax.optimization_barrier((value,) + others)[0]


def dot(left, right, left_dim, right_dim):
    return lax.dot_general(
        left, right, (((left_dim,), (right_dim,)), ((), ())), preferred_element_type=F32
    )


def cut_kernel(member_ref, up_ref, down_ref, *pieces):
    width = pieces[0].shape[2] // 2
    for at, step in enumerate(STEPS):
        for kind, source in enumerate((up_ref, down_ref)):
            for far in range(2):
                column = pl.multiple_of((far * 4 + (member_ref[0] ^ step)) * width, width)
                pieces[at][kind, :, far * width : (far + 1) * width] = source[:, pl.ds(column, width)]


def cut(member, up_rows, down_rows):
    units, features = up_rows.shape
    piece = jax.ShapeDtypeStruct((2, units, features // 4), BF16)
    return pl.pallas_call(
        cut_kernel,
        out_shape=[piece] * 4,
        in_specs=[pl.BlockSpec(memory_space=pltpu.SMEM)] + [pl.BlockSpec(memory_space=pltpu.VMEM)] * 2,
        out_specs=[pl.BlockSpec(memory_space=pltpu.VMEM)] * 4,
        compiler_params=pltpu.CompilerParams(vmem_limit_bytes=VMEM_BYTES),
        cost_estimate=pl.CostEstimate(flops=0, bytes_accessed=8 * units * features, transcendentals=0),
        name="cut_weights",
    )(member, up_rows, down_rows)


def lay_out_kernel(block_ref, column_ref, sent_ref):
    def rows_of(at, array):
        ends = [column_ref[end * 4 + at, array * 4 : array * 4 + 4].astype(F32) for end in range(2)]
        return jnp.concatenate(ends, axis=0).astype(BF16)

    for array in range(2):
        own = rows_of(block_ref[0], array)
        for near in range(2):
            blocks = [rows_of(far * 2 + near, array) for far in range(2)] + [own]
            for half in range(2):
                for line in range(4):
                    for far in range(3):
                        sent_ref[half * 8 + near * 4 + line, far, array] = blocks[far]


def lay_out(block, column):
    unused, rows, width = column.shape
    return pl.pallas_call(
        lay_out_kernel,
        out_shape=jax.ShapeDtypeStruct((16, 3, 2, rows, width), BF16),
        in_specs=[pl.BlockSpec(memory_space=pltpu.SMEM), pl.BlockSpec(memory_space=pltpu.VMEM)],
        out_specs=pl.BlockSpec(memory_space=pltpu.VMEM),
        compiler_params=pltpu.CompilerParams(vmem_limit_bytes=VMEM_BYTES),
        cost_estimate=pl.CostEstimate(flops=0, bytes_accessed=2_800_000, transcendentals=0),
        name="lay_out_rows",
    )(block, column)


def hidden_kernel(member_ref, source_ref, *refs):
    pieces, (out_ref, mine_ref, rows_ref, held_ref, sems) = refs[:8], refs[8:]
    units = pieces[0].shape[1]
    width = rows_ref.shape[4]
    copies = [pltpu.make_async_copy(source_ref, rows_ref, sems.at[8])]
    copies += [pltpu.make_async_copy(pieces[at], held_ref.at[at], sems.at[at]) for at in range(8)]
    for copy in copies:
        copy.start()
    copies[0].wait()
    for core in range(2):
        held = [held_ref.at[core * 4 + at] for at in range(4)]
        for copy in copies[1 + core * 4 : 5 + core * 4]:
            copy.wait()
        for kind in range(2):
            rows = [rows_ref[:, far, kind].reshape(-1, width) for far in range(2)]
            if core == 0:
                mine_ref[kind] = rows_ref[:, 2, kind].reshape(-1, width)
            total = None
            for far in range(2):
                weight = jnp.concatenate(
                    [piece[kind, :, far * width : (far + 1) * width] for piece in held], axis=0
                )
                term = dot(weight, rows[far], 1, 1)
                total = term if total is None else total + term
            sends = [(kind, total.astype(BF16))]
            if kind == 0:
                sends.append((2, (total - sends[0][1].astype(F32)).astype(BF16)))
            for row, value in sends:
                for place, step in enumerate(STEPS):
                    for at in range(4):
                        out_ref[at, member_ref[0] ^ step, row, core] = value[place * units : (place + 1) * units]


def hidden_parts(member, rows, own, beside):
    units = own[0].shape[1]
    tokens = rows.shape[0] * rows.shape[3]
    return pl.pallas_call(
        hidden_kernel,
        out_shape=[
            jax.ShapeDtypeStruct((4, 4, 3, 2, units, tokens), BF16),
            jax.ShapeDtypeStruct((2, tokens, rows.shape[4]), BF16),
        ],
        in_specs=[pl.BlockSpec(memory_space=pltpu.SMEM)] + [pl.BlockSpec(memory_space=pltpu.HBM)] * 9,
        out_specs=[pl.BlockSpec(memory_space=pltpu.VMEM)] * 2,
        scratch_shapes=[
            pltpu.VMEM(rows.shape, BF16),
            pltpu.VMEM((8,) + own[0].shape, BF16),
            pltpu.SemaphoreType.DMA((9,)),
        ],
        compiler_params=pltpu.CompilerParams(vmem_limit_bytes=3 * VMEM_BYTES),
        cost_estimate=pl.CostEstimate(flops=604_000_000, bytes_accessed=6_700_000, transcendentals=0),
        name="hidden_parts",
    )(member, rows, *own, *beside)


def output_kernel(member_ref, parts_ref, *refs):
    pieces, (out_ref, pair_ref, held_ref, sems) = refs[:8], refs[8:]
    copies = [pltpu.make_async_copy(pieces[at], held_ref.at[at], sems.at[at]) for at in range(8)]
    for copy in copies:
        copy.start()
    features = pieces[0].shape[2]
    count, unused, rows, unused = out_ref.shape
    step_of = features // 4
    units = [[], []]
    for core in range(2):
        for step in STEPS:
            slot = member_ref[0] ^ step
            value, act_grad, rest = (
                sum(parts_ref[source, slot, row, core].astype(F32) for source in range(4)) for row in range(3)
            )
            pre_act = value + rest
            values = (activate(pre_act).astype(BF16), gelu_slope(pre_act, act_grad).astype(BF16))
            for kind in range(2):
                units[kind].append(values[kind])
                if step < 2:
                    pair_ref[core, kind, 0, slot % 2] = values[kind]
    for copy in copies:
        copy.wait()
    for result in range(2):
        left = jnp.concatenate(units[result], axis=0)
        for cut_at in range(4):
            columns = slice(cut_at * step_of, (cut_at + 1) * step_of)
            weight = jnp.concatenate(
                [held_ref[at, 1 - result, :, columns] for at in range(8)], axis=0
            )
            total = dot(left, weight, 0, 0)
            out_ref[:, result, :, columns] = total.astype(BF16).reshape(count, rows, step_of)


def output_parts(member, parts, own, beside, count):
    features = own[0].shape[2]
    units, tokens = parts.shape[4:]
    return pl.pallas_call(
        output_kernel,
        out_shape=[
            jax.ShapeDtypeStruct((count, 2, tokens // count, features), BF16),
            jax.ShapeDtypeStruct((2, 2, 1, 2, units, tokens), BF16),
        ],
        in_specs=[pl.BlockSpec(memory_space=pltpu.SMEM), pl.BlockSpec(memory_space=pltpu.VMEM)]
        + [pl.BlockSpec(memory_space=pltpu.HBM)] * 8,
        out_specs=[pl.BlockSpec(memory_space=pltpu.VMEM)] * 2,
        scratch_shapes=[pltpu.VMEM((8,) + own[0].shape, BF16), pltpu.SemaphoreType.DMA((8,))],
        compiler_params=pltpu.CompilerParams(vmem_limit_bytes=3 * VMEM_BYTES),
        cost_estimate=pl.CostEstimate(flops=604_000_000, bytes_accessed=6_700_000, transcendentals=49_152),
        name="output_parts",
    )(member, parts, *own, *beside)


def sum_kernel(arrived_ref, out_ref):
    width = out_ref.shape[3]
    for near in range(2):
        for array in range(2):
            total = None
            for half in range(2):
                for line in range(4):
                    term = arrived_ref[half * 8 + near * 4 + line, array].astype(F32)
                    total = term if total is None else total + term
            for end in range(2):
                for far in range(2):
                    rows = total[end * 4 : end * 4 + 4, far * width : (far + 1) * width]
                    out_ref[end * 4 + far * 2 + near, array] = rows.astype(BF16)


def plane_sums(arrived):
    width = arrived.shape[3] // 2
    return pl.pallas_call(
        sum_kernel,
        out_shape=jax.ShapeDtypeStruct((8, 2, 4, width), BF16),
        in_specs=[pl.BlockSpec(memory_space=pltpu.VMEM)],
        out_specs=pl.BlockSpec(memory_space=pltpu.VMEM),
        compiler_params=pltpu.CompilerParams(vmem_limit_bytes=VMEM_BYTES),
        cost_estimate=pl.CostEstimate(flops=800_000, bytes_accessed=1_800_000, transcendentals=0),
        name="plane_sums",
    )(arrived)


def local(tokens, up_proj, down_proj, out_grad):
    width = tokens.shape[1]
    units = down_proj.shape[0]
    member = lax.axis_index(GROUP).reshape(1).astype(jnp.int32)

    pieces = cut(member, up_proj.T, down_proj)
    own = [pieces[0]] + [partner(pieces[at], GROUP, 4, STEPS[at]) for at in range(1, 4)]
    beside = [other_core(pieces[0])]
    waits = own[1:]
    for piece in own[1:]:
        beside.append(other_core(after(piece, *waits)))
        waits = beside[-1:]

    both = jnp.concatenate([tokens, out_grad], axis=0)
    column = spread(both, COLUMN, 8)
    block = lax.axis_index(("z2", "z1")).reshape(1).astype(jnp.int32)
    sent = lay_out(block, column)
    plane = exchange(sent, PLANE)

    parts, mine = hidden_parts(member, plane, own, beside)
    arrived = exchange(parts, GROUP)

    partials, pair = output_parts(member, arrived, own, beside, 16)
    arrived = exchange(partials, PLANE)
    summed = plane_sums(arrived)
    ends = jnp.sum(exchange(summed, COLUMN).astype(F32), axis=0).astype(BF16)

    flat = jnp.concatenate([mine, other_core(mine)], axis=1)
    lines = gather_ring(pair, ("z2", "z1"), 4, 2, arrived)
    lines = lines.reshape(2, 2, 8 * units, 128)
    units_all = jnp.concatenate([lines[0], other_core(lines[1])], axis=2)
    down_grad = dot(units_all[0], flat[1], 1, 0).astype(BF16)
    up_grad = dot(flat[0], units_all[1], 0, 1).astype(BF16)
    return (ends[0], ends[1], up_grad, down_grad)


def solution(mesh):
    fine = Mesh(
        mesh.devices.reshape(2, 2, 2, 4, 2, 2, 2, 2),
        ("xh", "xp", "zh", "y", "c", "z2", "z1", "zp"),
    )
    owners = ("xh", "xp", "zh", "y", "c")
    features = ("z2", "z1", "zp")
    return jax.shard_map(
        local,
        mesh=fine,
        in_specs=(
            P(owners, features),
            P(None, owners + features),
            P(owners + features, None),
            P(owners, features),
        ),
        out_specs=(
            P(owners, features),
            P(owners, features),
            P(features, owners),
            P(owners, features),
        ),
        check_vma=False,
    )
```
